512 devices in a mesh: tensor: 16 (over y, z_hi), context: 32 (over x, z_lo, core).
Axes of the slice: x: 4, y: 4, z: 16 (z_hi: 4, z_lo: 4; z = z_hi * 4 + z_lo), core: 2. Of those that a mesh axis runs over, the one named last changes fastest.
Arguments:
- projected: bfloat16 [3, 8192, 4096], P(None, 'tensor', 'context'), may hold values from -6 to 6
- short_weight: float32 [3, 8192, 3], P(None, 'tensor'), may hold values from -3.5 to 3.5
- residues: float32 [8192, 16], P(('tensor', 'context')), may hold values from -1.5 to 1.5
- decay_rates: float32 [8192, 16], P(('tensor', 'context')), may hold values from 0.5 to 128
- skip_weight: float32 [8192], P(('tensor', 'context')), may hold values from -3 to 3
- cotangent: bfloat16 [8192, 4096], P('tensor', 'context'), may hold values from -6 to 6
Outputs:
- output: bfloat16 [8192, 4096], P('tensor', 'context')
- grad_projected: bfloat16 [3, 8192, 4096], P(None, 'tensor', 'context')
- grad_short: float32 [3, 8192, 3], P(None, 'tensor')
- grad_residues: float32 [8192, 16], P(('tensor', 'context'))
- grad_decay: float32 [8192, 16], P(('tensor', 'context'))
- grad_skip: float32 [8192], P(('tensor', 'context'))
The draws below stay inside these ranges and needn't reach their ends.
All inputs are finite; a program needn't handle non-finite values.
Results may differ from the reference program's by a relative error of at most 0.0062.
Values may be sent and summed in bfloat16 or wider, within the bound.
A program may use at most 64 MiB of HBM per device.

```python
import math
import jax
import jax.numpy as jnp
from jax import lax

D = 8192
ORDER = 16
TAPS = 3
SEQ = 4096


def shard_levels(stream_key, extent, cuts, low, largest):
    factor_of, own = 1.0, jax.random.fold_in(stream_key, 6)
    for axis_at, blocks in cuts:
        heights = jnp.exp(jax.random.uniform(jax.random.fold_in(own, axis_at), (blocks,), jnp.float32, low / len(cuts), largest / len(cuts)))
        factor_of = factor_of * jnp.repeat(heights, extent[axis_at] // blocks).reshape([-1 if axis == axis_at else 1 for axis in range(len(extent))])
    return factor_of


def gaussian(stream_key, dims, deviation, reach, cuts=(), kind=jnp.bfloat16):
    level = shard_levels(stream_key, dims, cuts, -0.22, 0.18) if cuts else 1.0
    result = jax.random.normal(stream_key, dims, jnp.float32) * deviation * level
    return jnp.minimum(jnp.maximum(result, -reach), reach).astype(kind)


def setup_inputs(seed: int = 0) -> dict:
    splits = jax.random.split(jax.random.key(seed), 7)
    projected = gaussian(splits[0], (3, D, SEQ), 1.0, 6.0, ((1, 16), (2, 32)))
    short_weight = gaussian(splits[1], (3, D, TAPS), TAPS ** -0.5, 3.5, ((1, 16),), jnp.float32)
    residues = gaussian(splits[2], (D, ORDER), ORDER ** -0.5, 1.5, ((0, 512),), jnp.float32)
    decay_rates = jnp.clip(jnp.exp(math.log(128.0) - 5.5451774 * jax.random.uniform(splits[3], (D, ORDER), jnp.float32) ** shard_levels(splits[3], (D, ORDER), ((0, 512),), -0.2, 0.2)), 0.5, 128.0)
    skip_weight = gaussian(splits[4], (D,), 1.0, 3.0, ((0, 512),), jnp.float32)
    cotangent = gaussian(splits[5], (D, SEQ), 1.0, 6.0, ((0, 16), (1, 32)))
    return {"projected": projected, "short_weight": short_weight, "residues": residues, "decay_rates": decay_rates, "skip_weight": skip_weight, "cotangent": cotangent}


def mode_terms(decay_rates, length):
    per_step = decay_rates / length
    scales = jnp.sqrt(-jnp.expm1(-2.0 * per_step))
    return (per_step, scales)

def filter_taps(residues, per_step, scales, length):
    times = jnp.arange(length).astype(jnp.float32)
    coefs = residues * scales

    def add_mode(index, total):
        rate_col = lax.dynamic_slice_in_dim(per_step, index, 1, 1)
        coef_col = lax.dynamic_slice_in_dim(coefs, index, 1, 1)
        return total + coef_col * jnp.exp(-rate_col * times[None, :])
    start = jnp.zeros((residues.shape[0], length), jnp.float32)
    return lax.fori_loop(0, residues.shape[1], add_mode, start)

def mode_grads(grad_filter, residues, per_step, scales, length):
    times = jnp.arange(length).astype(jnp.float32)
    rates_rows = per_step.T

    def one_mode(rate_row):
        weights = jnp.exp(-rate_row[:, None] * times[None, :])
        plain = lax.optimization_barrier(jnp.sum(grad_filter * weights, axis=1))
        ramped = lax.optimization_barrier(jnp.sum(grad_filter * weights * times[None, :], axis=1))
        return jnp.stack([plain, ramped])
    sums = lax.map(one_mode, rates_rows)
    plain = sums[:, 0, :].T
    ramped = sums[:, 1, :].T
    root = math.sqrt(length)
    grad_residues = scales * plain / root
    grad_decay = residues * (jnp.exp(-2.0 * per_step) / scales * plain - scales * ramped) / (length * root)
    return (grad_residues, grad_decay)

def reference(projected, short_weight, residues, decay_rates, skip_weight, cotangent):
    length = projected.shape[2]
    tap_count = short_weight.shape[2]
    channels = projected.shape[1]
    proj_float = projected.astype(jnp.float32)
    padded = jnp.pad(proj_float, ((0, 0), (0, 0), (tap_count - 1, 0)))
    filtered = jnp.zeros(proj_float.shape, jnp.float32)
    for offset in range(tap_count):
        start = tap_count - 1 - offset
        filtered = filtered + short_weight[:, :, offset:offset + 1] * padded[:, :, start:start + length]
    query_path = filtered[0]
    key_path = filtered[1]
    value_path = filtered[2]
    gated_signal = (key_path * value_path).astype(jnp.bfloat16)
    cot_float = cotangent.astype(jnp.float32)
    grad_conv = (cot_float * query_path).astype(jnp.bfloat16)
    block = 256
    count = channels // block
    size = 2 * length
    root = math.sqrt(length)

    def block_work(pieces):
        gated_blk, grad_blk, res_blk, rate_blk, skip_blk = pieces
        per_step, scales = mode_terms(rate_blk, length)
        taps = filter_taps(res_blk, per_step, scales, length)
        spec_taps = jnp.fft.rfft(taps, n=size)
        gated_float = gated_blk.astype(jnp.float32)
        grad_float = grad_blk.astype(jnp.float32)
        spec_gated = jnp.fft.rfft(gated_float, n=size)
        spec_grad = jnp.fft.rfft(grad_float, n=size)
        conv_blk = jnp.fft.irfft(spec_gated * spec_taps, n=size)[:, :length] + skip_blk[:, None] * gated_float
        back_blk = jnp.fft.irfft(spec_grad * jnp.conj(spec_taps), n=size)[:, :length] + skip_blk[:, None] * grad_float
        grad_filter = jnp.fft.irfft(spec_grad * jnp.conj(spec_gated), n=size)[:, :length]
        grad_skip = lax.optimization_barrier(jnp.sum(grad_float * gated_float, axis=1)) / root
        grad_res, grad_dec = mode_grads(grad_filter, res_blk, per_step, scales, length)
        return (conv_blk.astype(jnp.bfloat16), back_blk.astype(jnp.bfloat16), grad_res, grad_dec, grad_skip)
    results = lax.map(block_work, (gated_signal.reshape(count, block, length), grad_conv.reshape(count, block, length), residues.reshape(count, block, -1), decay_rates.reshape(count, block, -1), skip_weight.reshape(count, block)))
    conv_out = results[0].reshape(channels, length)
    grad_signal = results[1].reshape(channels, length)
    grad_residues = results[2].reshape(channels, -1)
    grad_decay = results[3].reshape(channels, -1)
    grad_skip = results[4].reshape(channels)
    conv_float = conv_out.astype(jnp.float32)
    output = (query_path * conv_float).astype(jnp.bfloat16)
    signal_float = grad_signal.astype(jnp.float32)
    grad_filtered = jnp.stack([cot_float * conv_float, signal_float * value_path, signal_float * key_path])
    padded_grad = jnp.pad(grad_filtered, ((0, 0), (0, 0), (0, tap_count - 1)))
    grad_projected = jnp.zeros(grad_filtered.shape, jnp.float32)
    for offset in range(tap_count):
        grad_projected = grad_projected + short_weight[:, :, offset:offset + 1] * padded_grad[:, :, offset:offset + length]
    grad_projected = grad_projected.astype(jnp.bfloat16)
    columns = []
    for offset in range(tap_count):
        start = tap_count - 1 - offset
        columns.append(lax.optimization_barrier(jnp.sum(grad_filtered * padded[:, :, start:start + length], axis=2)))
    grad_short = jnp.stack(columns, axis=2) / root
    return (output, grad_projected, grad_short, grad_residues, grad_decay, grad_skip)
```

```python
import functools
import math

import jax
import jax.numpy as jnp
from jax import lax
from jax.experimental import pallas as pl
from jax.experimental.pallas import tpu as pltpu
from jax.sharding import PartitionSpec as P

MESH = pl.DeviceIdType.MESH
SUB = 8
MODES = 16
TAPS = 3
OFF = 8
F32 = jnp.float32


def rounded(value):
    return value.astype(jnp.bfloat16).astype(F32)


def one_minus_exp(x):
    series = jnp.ones_like(x)
    for k in range(10, 1, -1):
        series = 1.0 - x * (1.0 / k) * series
    return jnp.where(x < 0.5, x * series, 1.0 - jnp.exp(-x))


def kernel(
    n,
    local_len,
    own,
    proj_ref,
    cot_ref,
    sw_ref,
    decay_ref,
    res_ref,
    skip_ref,
    out_ref,
    gproj_ref,
    gshort_ref,
    gres_ref,
    gdec_ref,
    gskip_ref,
    rx,
    xt,
    qs,
    ks,
    vs,
    us,
    gs,
    ys,
    zs,
    gf,
    ot,
    so,
    gsend,
    grecv,
    par,
    wt,
    lam,
    coef,
    tots,
    sin,
    pacc,
    racc,
    send_sem,
    recv_sem,
    own_sem,
):
    me = lax.axis_index("context")
    length = n * local_len
    steps = local_len // SUB
    groups = 128 // own
    tiles = n // groups
    root = math.sqrt(length)

    def peer_at(t):
        return lax.rem(me + t, n)

    def each_peer(body):
        def step(t, carry):
            body(peer_at(t))
            return carry

        lax.fori_loop(1, n, step, 0)

    barrier = pltpu.get_barrier_semaphore()
    each_peer(
        lambda p: pl.semaphore_signal(
            barrier, inc=1, device_id={"context": p}, device_id_type=MESH
        )
    )

    lane = lax.broadcasted_iota(jnp.int32, (1, 128), 1)
    group = lane // own
    sub_row = lax.broadcasted_iota(jnp.int32, (SUB, 128), 0)

    def spread(row):
        row = jnp.where(lane < own, row, 0.0)
        width = own
        while width < 128:
            row = row + pltpu.roll(row, width, 1)
            width *= 2
        return row

    def group_sum(rows):
        width = own
        while width < 128:
            rows = rows + pltpu.roll(rows, width, 1)
            width *= 2
        return rows

    par[...] = jnp.zeros_like(par)
    for g in range(groups):
        par[0, g * own : (g + 1) * own, 0:MODES] = decay_ref[...]
        par[1, g * own : (g + 1) * own, 0:MODES] = res_ref[...]
    per = par[0].T[0:MODES, :] * (1.0 / length)
    residue = par[1].T[0:MODES, :]
    scale = jnp.sqrt(one_minus_exp(2.0 * per))
    coef_rows = residue * scale
    lam_rows = jnp.exp(-per)
    par[2, 0:MODES, :] = per
    for m in range(MODES):
        lam[m] = jnp.broadcast_to(lam_rows[m : m + 1, :], (SUB, 128))
        coef[m] = jnp.broadcast_to(coef_rows[m : m + 1, :], (SUB, 128))
    first_lane = pl.multiple_of((me // groups) * 128, 128)
    shift = lax.rem(128 - lax.rem(me, groups) * own, 128)
    for i in range(3):
        rows = pltpu.roll(
            jnp.concatenate(
                [sw_ref[i, :, pl.ds(first_lane, 128)], jnp.zeros((SUB - TAPS, 128), F32)], axis=0
            ),
            shift,
            1,
        )
        for j in range(TAPS):
            wt[TAPS * i + j] = jnp.broadcast_to(spread(rows[j : j + 1, :]), (SUB, 128))
    par[3, 0:1, 0:own] = skip_ref[...]
    wt[9] = jnp.broadcast_to(spread(par[3, 0:1, :]), (SUB, 128))

    pl.semaphore_wait(barrier, n - 1)

    def send_inputs(p):
        rows = pl.ds(pl.multiple_of(p * own, own), own)
        pltpu.make_async_remote_copy(
            src_ref=proj_ref.at[:, rows, :],
            dst_ref=rx.at[me, pl.ds(0, 3)],
            send_sem=send_sem.at[0],
            recv_sem=recv_sem.at[0],
            device_id={"context": p},
            device_id_type=MESH,
        ).start()
        pltpu.make_async_remote_copy(
            src_ref=cot_ref.at[rows, :],
            dst_ref=rx.at[me, 3],
            send_sem=send_sem.at[1],
            recv_sem=recv_sem.at[1],
            device_id={"context": p},
            device_id_type=MESH,
        ).start()

    each_peer(send_inputs)
    my_rows = pl.ds(pl.multiple_of(me * own, own), own)
    keep_proj = pltpu.make_async_copy(
        proj_ref.at[:, my_rows, :], rx.at[me, pl.ds(0, 3)], own_sem.at[0]
    )
    keep_cot = pltpu.make_async_copy(cot_ref.at[my_rows, :], rx.at[me, 3], own_sem.at[1])
    keep_proj.start()
    keep_cot.start()
    keep_proj.wait()
    keep_cot.wait()
    others = pl.ds(0, n - 1)
    all_proj = rx.at[others, pl.ds(0, 3)]
    all_cot = rx.at[others, 3]
    pltpu.make_async_copy(all_proj, all_proj, recv_sem.at[0]).wait()
    pltpu.make_async_copy(all_cot, all_cot, recv_sem.at[1]).wait()

    def turn(jt, carry):
        for a in range(4):
            block = rx[pl.ds(groups * jt, groups), a].reshape(128, local_len).astype(F32)
            xt[a, jt, OFF : OFF + local_len, :] = block.T
        return carry

    lax.fori_loop(0, tiles, turn, 0)
    for a in range(3):
        for jt in range(tiles):
            before = pltpu.roll(xt[a, jt, OFF + local_len - 8 : OFF + local_len, :], own, 1)
            if jt:
                last = pltpu.roll(xt[a, jt - 1, OFF + local_len - 8 : OFF + local_len, :], own, 1)
            else:
                last = jnp.zeros((8, 128), F32)
            xt[a, jt, 0:8, :] = jnp.where(group == 0, last, before)

    def gates(jt, carry):
        for p in range(steps):
            paths = []
            for a in range(3):
                total = None
                for j in range(TAPS):
                    rows = xt[a, jt, pl.ds(OFF + p - j, SUB, stride=steps), :]
                    term = wt[TAPS * a + j] * rows
                    total = term if total is None else total + term
                paths.append(total)
            query, key, value = paths
            qs[jt, p] = query
            ks[jt, p] = key
            vs[jt, p] = value
            us[jt, p] = rounded(key * value)
            gs[jt, p] = rounded(xt[3, jt, pl.ds(OFF + p, SUB, stride=steps), :] * query)
        return carry

    lax.fori_loop(0, tiles, gates, 0)

    many = 4

    def ends(at, carry):
        jt = at // (MODES // many)
        first = lax.rem(at, MODES // many) * many
        lams = [lam[first + i] for i in range(many)]
        fwd = [None] * many
        bwd = [None] * many
        for p in range(steps):
            u = us[jt, p]
            g = gs[jt, steps - 1 - p]
            for i in range(many):
                fwd[i] = u if fwd[i] is None else lams[i] * fwd[i] + u
                bwd[i] = g if bwd[i] is None else lams[i] * bwd[i] + g
        for i in range(many):
            pers = jnp.broadcast_to(par[2, pl.ds(first + i, 1), :], (SUB, 128))
            f, b = fwd[i], bwd[i]
            for k in (1, 2, 4):
                factor = jnp.exp(pers * (-1.0 * steps * k))
                f = f + factor * jnp.where(sub_row >= k, pltpu.roll(f, k, 0), 0.0)
                b = b + factor * jnp.where(sub_row < SUB - k, pltpu.roll(b, SUB - k, 0), 0.0)
            sin[0, jt, first + i] = f
            sin[1, jt, first + i] = b
            tots[0, jt, pl.ds(first + i, 1), :] = f[SUB - 1 : SUB, :]
            tots[1, jt, pl.ds(first + i, 1), :] = b[0:1, :]
        return carry

    lax.fori_loop(0, tiles * (MODES // many), ends, 0)

    per_all = par[2, 0:MODES, :]
    spans = [jnp.exp(per_all * (-1.0 * local_len * k)) for k in (1, 2, 4)]
    tile_span = jnp.exp(per_all * (-1.0 * local_len * groups))
    up_span = jnp.exp(per_all * (-1.0 * local_len) * group.astype(F32))
    down_span = jnp.exp(per_all * (-1.0 * local_len) * (groups - 1 - group).astype(F32))
    carry_f = jnp.zeros((MODES, 128), F32)
    for jt in range(tiles):
        f = tots[0, jt]
        for k, span in zip((1, 2, 4), spans):
            f = f + span * jnp.where(group >= k, pltpu.roll(f, own * k, 1), 0.0)
        before = jnp.where(group >= 1, pltpu.roll(f, own, 1), 0.0)
        tots[0, jt] = before + up_span * carry_f
        last = group_sum(jnp.where(group == groups - 1, f, 0.0))
        carry_f = tile_span * carry_f + last
    carry_b = jnp.zeros((MODES, 128), F32)
    for jt in reversed(range(tiles)):
        b = tots[1, jt]
        for k, span in zip((1, 2, 4), spans):
            b = b + span * jnp.where(group < groups - k, pltpu.roll(b, 128 - own * k, 1), 0.0)
        after = jnp.where(group < groups - 1, pltpu.roll(b, 128 - own, 1), 0.0)
        tots[1, jt] = after + down_span * carry_b
        head = group_sum(jnp.where(group == 0, b, 0.0))
        carry_b = tile_span * carry_b + head

    ys[...] = jnp.zeros_like(ys)
    zs[...] = jnp.zeros_like(zs)
    pacc[...] = jnp.zeros_like(pacc)
    racc[...] = jnp.zeros_like(racc)
    pair = 2

    def modes(at, carry):
        jt = at // (MODES // pair)
        first = lax.rem(at, MODES // pair) * pair
        lams, coefs, f_in, b_in = [], [], [], []
        for i in range(pair):
            m = first + i
            pers = jnp.broadcast_to(par[2, pl.ds(m, 1), :], (SUB, 128))
            sub_f = sub_row.astype(F32)
            f = sin[0, jt, m]
            b = sin[1, jt, m]
            f = jnp.where(sub_row >= 1, pltpu.roll(f, 1, 0), 0.0) + jnp.exp(
                pers * (-1.0 * steps) * sub_f
            ) * jnp.broadcast_to(tots[0, jt, pl.ds(m, 1), :], (SUB, 128))
            b = jnp.where(sub_row < SUB - 1, pltpu.roll(b, SUB - 1, 0), 0.0) + jnp.exp(
                pers * (-1.0 * steps) * (SUB - 1 - sub_f)
            ) * jnp.broadcast_to(tots[1, jt, pl.ds(m, 1), :], (SUB, 128))
            f_in.append(f)
            b_in.append(b)
            lams.append(lam[m])
            coefs.append(coef[m])
        behind = [[None] * (steps + 1) for _ in range(pair)]
        for i in range(pair):
            behind[i][steps] = b_in[i]
        for p in reversed(range(steps)):
            g = gs[jt, p]
            z = zs[jt, p]
            for i in range(pair):
                now = lams[i] * behind[i][p + 1] + g
                behind[i][p] = now
                z = z + coefs[i] * now
            zs[jt, p] = z
        plain = [None] * pair
        ramped = [None] * pair
        state = f_in
        for p in range(steps):
            u = us[jt, p]
            g = gs[jt, p]
            y = ys[jt, p]
            for i in range(pair):
                state[i] = lams[i] * state[i] + u
                y = y + coefs[i] * state[i]
                flat = g * state[i]
                ramp = behind[i][p + 1] * state[i]
                plain[i] = flat if plain[i] is None else plain[i] + flat
                ramped[i] = ramp if ramped[i] is None else ramped[i] + ramp
            ys[jt, p] = y
        for i in range(pair):
            pacc[first + i] += plain[i]
            racc[first + i] += ramped[i]
        return carry

    lax.fori_loop(0, tiles * (MODES // pair), modes, 0)

    def paths_grads(jt, skip_total):
        skip = wt[9]
        for p in range(steps):
            u = us[jt, p]
            g = gs[jt, p]
            conv = rounded(ys[jt, p] + skip * u)
            back = rounded(zs[jt, p] + skip * g)
            at = pl.ds(p, SUB, stride=steps)
            ot[0, jt, at, :] = qs[jt, p] * conv
            gf[0, jt, at, :] = xt[3, jt, pl.ds(OFF + p, SUB, stride=steps), :] * conv
            gf[1, jt, at, :] = back * vs[jt, p]
            gf[2, jt, at, :] = back * ks[jt, p]
            skip_total = skip_total + u * g
        return skip_total

    skip_total = lax.fori_loop(0, tiles, paths_grads, jnp.zeros((SUB, 128), F32))
    for a in range(3):
        for jt in range(tiles):
            after = pltpu.roll(gf[a, jt, 0:8, :], 128 - own, 1)
            if jt + 1 < tiles:
                head = pltpu.roll(gf[a, jt + 1, 0:8, :], 128 - own, 1)
            else:
                head = jnp.zeros((8, 128), F32)
            gf[a, jt, local_len : local_len + 8, :] = jnp.where(group == groups - 1, head, after)

    def finish(jt, carry):
        so[pl.ds(groups * jt, groups), 0] = (
            ot[0, jt].T.astype(jnp.bfloat16).reshape(groups, own, local_len)
        )
        totals = []
        for a in range(3):
            total = None
            for j in range(TAPS):
                w = jnp.broadcast_to(wt[TAPS * a + j][0:1, :], (local_len, 128))
                term = w * gf[a, jt, j : j + local_len, :]
                total = term if total is None else total + term
                totals.append(
                    carry[TAPS * a + j]
                    + jnp.sum(
                        gf[a, jt, 0:local_len, :] * xt[a, jt, OFF - j : OFF - j + local_len, :],
                        axis=0,
                        keepdims=True,
                    )
                )
            so[pl.ds(groups * jt, groups), 1 + a] = (
                total.T.astype(jnp.bfloat16).reshape(groups, own, local_len)
            )
        return tuple(totals)

    short = lax.fori_loop(0, tiles, finish, tuple(jnp.zeros((1, 128), F32) for _ in range(9)))
    mine = group == lax.rem(me, groups)
    gsend[...] = jnp.zeros_like(gsend)
    for r in range(9):
        gsend[r : r + 1, :] = jnp.where(mine, group_sum(short[r]), 0.0) * (1.0 / root)

    def send_results(p):
        pltpu.make_async_remote_copy(
            src_ref=so.at[p, 0],
            dst_ref=out_ref.at[my_rows, :],
            send_sem=send_sem.at[2],
            recv_sem=recv_sem.at[2],
            device_id={"context": p},
            device_id_type=MESH,
        ).start()
        pltpu.make_async_remote_copy(
            src_ref=so.at[p, pl.ds(1, 3)],
            dst_ref=gproj_ref.at[:, my_rows, :],
            send_sem=send_sem.at[3],
            recv_sem=recv_sem.at[3],
            device_id={"context": p},
            device_id_type=MESH,
        ).start()
        pltpu.make_async_remote_copy(
            src_ref=gsend,
            dst_ref=grecv.at[me],
            send_sem=send_sem.at[4],
            recv_sem=recv_sem.at[4],
            device_id={"context": p},
            device_id_type=MESH,
        ).start()

    each_peer(send_results)
    keep_out = pltpu.make_async_copy(so.at[me, 0], out_ref.at[my_rows, :], own_sem.at[0])
    keep_gp = pltpu.make_async_copy(
        so.at[me, pl.ds(1, 3)], gproj_ref.at[:, my_rows, :], own_sem.at[1]
    )
    keep_out.start()
    keep_gp.start()
    grecv[me] = gsend[...]

    plain = jnp.concatenate(
        [jnp.sum(pacc[m], axis=0, keepdims=True) for m in range(MODES)], axis=0
    )
    ramped = jnp.concatenate(
        [jnp.sum(racc[m], axis=0, keepdims=True) for m in range(MODES)], axis=0
    )
    plain = group_sum(plain)
    ramped = lam_rows * group_sum(ramped)
    grad_res = scale * plain / root
    grad_dec = (
        residue * (jnp.exp(-2.0 * per_all) / scale * plain - scale * ramped) / (length * root)
    )
    par[0, 0:MODES, :] = grad_res
    par[1, 0:MODES, :] = grad_dec
    gres_ref[...] = par[0].T[0:own, 0:MODES]
    gdec_ref[...] = par[1].T[0:own, 0:MODES]
    gskip_ref[...] = (
        group_sum(jnp.sum(skip_total, axis=0, keepdims=True))[:, 0:own] * (1.0 / root)
    )

    pltpu.make_async_copy(grecv.at[others], grecv.at[others], recv_sem.at[4]).wait()
    for jt in range(tiles):
        total = grecv[groups * jt]
        for g in range(1, groups):
            total = total + grecv[groups * jt + g]
        for i in range(3):
            gshort_ref[i, :, 128 * jt : 128 * (jt + 1)] = total[TAPS * i : TAPS * (i + 1), :]
    keep_out.wait()
    keep_gp.wait()
    most = pl.ds(0, (n - 1) * own)
    pltpu.make_async_copy(out_ref.at[most, :], out_ref.at[most, :], recv_sem.at[2]).wait()
    pltpu.make_async_copy(
        gproj_ref.at[:, most, :], gproj_ref.at[:, most, :], recv_sem.at[3]
    ).wait()
    pltpu.make_async_copy(all_proj, all_proj, send_sem.at[0]).wait()
    pltpu.make_async_copy(all_cot, all_cot, send_sem.at[1]).wait()
    pltpu.make_async_copy(so.at[others, 0], so.at[others, 0], send_sem.at[2]).wait()
    sent = so.at[others, pl.ds(1, 3)]
    pltpu.make_async_copy(sent, sent, send_sem.at[3]).wait()
    pltpu.make_async_copy(grecv.at[others], grecv.at[others], send_sem.at[4]).wait()


def per_device(projected, short_weight, residues, decay_rates, skip_weight, cotangent):
    n = lax.axis_size("context")
    channels, local_len = cotangent.shape
    own = channels // n
    tiles = n // (128 // own)
    steps = local_len // SUB
    vmem = pl.BlockSpec(memory_space=pltpu.VMEM)
    anywhere = pl.BlockSpec(memory_space=pl.ANY)
    stepped = pltpu.VMEM((tiles, steps, SUB, 128), F32)
    results = pl.pallas_call(
        functools.partial(kernel, n, local_len, own),
        out_shape=(
            jax.ShapeDtypeStruct((channels, local_len), jnp.bfloat16),
            jax.ShapeDtypeStruct((3, channels, local_len), jnp.bfloat16),
            jax.ShapeDtypeStruct((3, TAPS, channels), F32),
            jax.ShapeDtypeStruct((own, MODES), F32),
            jax.ShapeDtypeStruct((own, MODES), F32),
            jax.ShapeDtypeStruct((1, own), F32),
        ),
        in_specs=[anywhere, anywhere, vmem, vmem, vmem, vmem],
        out_specs=(anywhere, anywhere, vmem, vmem, vmem, vmem),
        scratch_shapes=[
            pltpu.VMEM((n, 4, own, local_len), jnp.bfloat16),
            pltpu.VMEM((4, tiles, OFF + local_len, 128), F32),
            stepped,
            stepped,
            stepped,
            stepped,
            stepped,
            stepped,
            stepped,
            pltpu.VMEM((3, tiles, local_len + 8, 128), F32),
            pltpu.VMEM((1, tiles, local_len, 128), F32),
            pltpu.VMEM((n, 4, own, local_len), jnp.bfloat16),
            pltpu.VMEM((16, 128), F32),
            pltpu.VMEM((n, 16, 128), F32),
            pltpu.VMEM((4, 128, 128), F32),
            pltpu.VMEM((10, SUB, 128), F32),
            pltpu.VMEM((MODES, SUB, 128), F32),
            pltpu.VMEM((MODES, SUB, 128), F32),
            pltpu.VMEM((2, tiles, MODES, 128), F32),
            pltpu.VMEM((2, tiles, MODES, SUB, 128), F32),
            pltpu.VMEM((MODES, SUB, 128), F32),
            pltpu.VMEM((MODES, SUB, 128), F32),
            pltpu.SemaphoreType.DMA((5,)),
            pltpu.SemaphoreType.DMA((5,)),
            pltpu.SemaphoreType.DMA((2,)),
        ],
        compiler_params=pltpu.CompilerParams(
            collective_id=0, has_side_effects=True, vmem_limit_bytes=32 * 1024 * 1024
        ),
    )(
        projected,
        cotangent,
        short_weight.transpose(0, 2, 1),
        decay_rates,
        residues,
        skip_weight.reshape(1, -1),
    )
    output, grad_projected, grad_short, grad_res, grad_dec, grad_skip = results
    return (
        output,
        grad_projected,
        grad_short.transpose(0, 2, 1),
        grad_res,
        grad_dec,
        grad_skip.reshape(-1),
    )


def solution(mesh):
    return jax.shard_map(
        per_device,
        mesh=mesh,
        in_specs=(
            P(None, "tensor", "context"),
            P(None, "tensor", None),
            P(("tensor", "context"), None),
            P(("tensor", "context"), None),
            P(("tensor", "context")),
            P("tensor", "context"),
        ),
        out_specs=(
            P("tensor", "context"),
            P(None, "tensor", "context"),
            P(None, "tensor", None),
            P(("tensor", "context"), None),
            P(("tensor", "context"), None),
            P(("tensor", "context")),
        ),
        check_vma=False,
    )
```

```python
import functools
import math

import jax
import jax.numpy as jnp
from jax import lax
from jax.experimental import pallas as pl
from jax.experimental.pallas import tpu as pltpu
from jax.sharding import PartitionSpec as P

MESH = pl.DeviceIdType.MESH
SUB = 8
MODES = 16
TAPS = 3
OFF = 8
RUNS = 4
WIDE = 4
HALF = RUNS * WIDE
F32 = jnp.float32
BF16 = jnp.bfloat16


def rounded(value):
    return value.astype(BF16).astype(F32)


def one_minus_exp(x):
    series = jnp.ones_like(x)
    for k in range(10, 1, -1):
        series = 1.0 - x * (1.0 / k) * series
    return jnp.where(x < 0.5, x * series, 1.0 - jnp.exp(-x))


def kernel(
    n,
    local_len,
    own,
    proj_ref,
    cot_ref,
    sw_hbm,
    decay_hbm,
    res_hbm,
    skip_hbm,
    out_ref,
    gproj_ref,
    gshort_ref,
    gres_ref,
    gdec_ref,
    gskip_ref,
    rx,
    so,
    xt,
    qs,
    ks,
    vs,
    us,
    gs,
    cv,
    gf,
    ot,
    sw,
    filt,
    par,
    wt,
    lam,
    coef,
    tots,
    ins,
    ends,
    edge,
    edge_in,
    sums,
    sums_in,
    shorts,
    all_short,
    pacc,
    racc,
    send_sem,
    recv_sem,
    local_sem,
):
    me = lax.axis_index("context")
    length = n * local_len
    steps = local_len // SUB
    chans = 2 * own
    root = math.sqrt(length)
    run_len = WIDE * local_len
    side = lax.rem(me // WIDE, 2)
    my_x = me // (2 * WIDE)
    my_w = lax.rem(me, WIDE)
    my_slot = my_x * WIDE + my_w
    partner = me + WIDE * (1 - 2 * side)
    is_a = side == 0

    def each_peer(body):
        def step(t, carry):
            slot = lax.rem(my_slot + t, HALF)
            x, w = slot // WIDE, lax.rem(slot, WIDE)
            body(slot, x, w, (2 * x + side) * WIDE + w)
            return carry

        lax.fori_loop(1, HALF, step, 0)

    def remote(src, dst, k, device):
        return pltpu.make_async_remote_copy(
            src_ref=src,
            dst_ref=dst,
            send_sem=send_sem.at[k],
            recv_sem=recv_sem.at[k],
            device_id={"context": device},
            device_id_type=MESH,
        )

    def arrived(ref, k):
        pltpu.make_async_copy(ref, ref, recv_sem.at[k]).wait()

    def left(ref, k):
        pltpu.make_async_copy(ref, ref, send_sem.at[k]).wait()

    barrier = pltpu.get_barrier_semaphore()
    pl.semaphore_signal(barrier, inc=1, device_id={"context": partner}, device_id_type=MESH)
    each_peer(
        lambda slot, x, w, device: pl.semaphore_signal(
            barrier, inc=1, device_id={"context": device}, device_id_type=MESH
        )
    )
    small = [
        pltpu.make_async_copy(sw_hbm, sw, local_sem.at[0]),
        pltpu.make_async_copy(decay_hbm, filt.at[0], local_sem.at[1]),
        pltpu.make_async_copy(res_hbm, filt.at[1], local_sem.at[2]),
        pltpu.make_async_copy(skip_hbm, filt.at[2, pl.ds(0, 1)], local_sem.at[3]),
    ]
    keep = [
        pltpu.make_async_copy(
            proj_ref.at[:, my_x, :, my_w], rx.at[my_slot, pl.ds(0, 3)], local_sem.at[4]
        ),
        pltpu.make_async_copy(cot_ref.at[my_x, :, my_w], rx.at[my_slot, 3], local_sem.at[5]),
    ]
    for copy in small + keep:
        copy.start()

    lane = lax.broadcasted_iota(jnp.int32, (1, 128), 1)
    group = lane // chans
    sub_row = lax.broadcasted_iota(jnp.int32, (SUB, 128), 0)
    corner = jnp.logical_and(sub_row == 0, group == 0)

    def group_sum(rows):
        width = chans
        while width < 128:
            rows = rows + pltpu.roll(rows, width, 1)
            width *= 2
        return rows

    def to_group(rows, here, there):
        shift = ((there - here) * chans) % 128
        return pltpu.roll(rows, shift, 1) if shift else rows

    def packed(tiles, here):
        total = None
        for jt in range(RUNS):
            piece = jnp.where(group == jt, to_group(tiles[jt], here, jt), 0.0)
            total = piece if total is None else total + piece
        return total

    def repeated(rows, jt):
        return group_sum(jnp.where(group == jt, rows, 0.0))

    def before(rows):
        return jnp.where(group >= 1, pltpu.roll(rows, chans, 1), 0.0)

    def after(rows):
        return jnp.where(group < RUNS - 1, pltpu.roll(rows, 128 - chans, 1), 0.0)

    for copy in small:
        copy.wait()
    pl.semaphore_wait(barrier, HALF)

    remote(filt.at[pl.ds(0, 3)], filt.at[pl.ds(3, 3)], 3, partner).start()

    def send_kv(slot, x, w, device):
        remote(proj_ref.at[pl.ds(1, 2), x, :, w], rx.at[my_slot, pl.ds(1, 2)], 0, device).start()

    def send_q_cot(slot, x, w, device):
        remote(proj_ref.at[0, x, :, w], rx.at[my_slot, 0], 1, device).start()
        remote(cot_ref.at[x, :, w], rx.at[my_slot, 3], 2, device).start()

    each_peer(send_kv)
    each_peer(send_q_cot)

    for i in range(3):
        rows = jnp.concatenate(
            [
                sw[i, :, pl.ds(pl.multiple_of(my_x * 128, 128), 128)],
                jnp.zeros((SUB - TAPS, 128), F32),
            ],
            axis=0,
        )
        rows = pltpu.roll(rows, lax.rem(128 - my_w * own, 128), 1)
        rows = jnp.where(lane < own, rows, 0.0) + pltpu.roll(
            jnp.where(jnp.logical_and(lane >= 64, lane < 64 + own), rows, 0.0), 64 + own, 1
        )
        rows = group_sum(rows)
        for j in range(TAPS):
            wt[TAPS * i + j] = jnp.broadcast_to(rows[j : j + 1, :], (SUB, 128))
    for copy in keep:
        copy.wait()
    arrived(filt.at[pl.ds(3, 3)], 3)
    par[...] = jnp.zeros_like(par)
    for k in range(2):
        mine, theirs = filt[k], filt[3 + k]
        first, second = jnp.where(is_a, mine, theirs), jnp.where(is_a, theirs, mine)
        for g in range(128 // chans):
            par[k, g * chans : g * chans + own, 0:MODES] = first
            par[k, g * chans + own : (g + 1) * chans, 0:MODES] = second
    mine, theirs = filt[2, 0:1, :], filt[5, 0:1, :]
    par[2, 0:1, 0:own] = jnp.where(is_a, mine, theirs)
    par[2, 1:2, 0:own] = jnp.where(is_a, theirs, mine)
    skip_row = group_sum(par[2, 0:1, :] + pltpu.roll(par[2, 1:2, :], own, 1))
    wt[9] = jnp.broadcast_to(skip_row, (SUB, 128))
    per = par[0].T[0:MODES, :] * (1.0 / length)
    residue = par[1].T[0:MODES, :]
    scale = jnp.sqrt(one_minus_exp(2.0 * per))
    coef_rows = residue * scale
    lam_rows = jnp.exp(-per)
    inv_lam = jnp.exp(per)
    par[3, 0:MODES, :] = per
    for m in range(MODES):
        lam[m] = jnp.broadcast_to(lam_rows[m : m + 1, :], (SUB, 128))
        coef[m] = jnp.broadcast_to(coef_rows[m : m + 1, :], (SUB, 128))

    def power(span):
        return jnp.exp(per * (-1.0 * span))

    sub_spans = [1, 2, 4]
    run_span, pair_span = power(run_len), power(2 * run_len)
    up_span = jnp.exp(per * (-1.0 * local_len) * group.astype(F32))
    down_span = jnp.exp(per * (-1.0 * local_len) * (WIDE - 1 - group).astype(F32))

    def turn(arrays):
        def tile(jt, carry):
            for a in arrays:
                block = rx[pl.ds(WIDE * jt, WIDE), a].reshape(128, local_len).astype(F32)
                turned = block.T
                xt[a, jt, OFF : OFF + local_len, :] = turned
                if a < 3:
                    xt[a, jt, 0:OFF, :] = jnp.where(
                        group == 0, 0.0, pltpu.roll(turned[local_len - OFF :, :], chans, 1)
                    )
            return carry

        lax.fori_loop(0, RUNS, tile, 0)

    def path(a, jt, p):
        total = None
        for j in range(TAPS):
            term = wt[TAPS * a + j] * xt[a, jt, pl.ds(OFF + p - j, SUB, stride=steps), :]
            total = term if total is None else total + term
        return total

    def last_rows(a):
        return packed(
            [xt[a, jt, OFF + local_len - 8 : OFF + local_len, :] for jt in range(RUNS)], WIDE - 1
        )[6:8, :]

    def first_rows(a):
        return packed([xt[a, jt, OFF : OFF + 8, :] for jt in range(RUNS)], 0)[0:2, :]

    def edge_path(a, first, last):
        w = [wt[TAPS * a + j][0:1, :] for j in range(TAPS)]
        return (
            w[0] * first[0:1] + w[1] * last[1:2] + w[2] * last[0:1],
            w[0] * first[1:2] + w[1] * first[0:1] + w[2] * last[1:2],
        )

    def mine_before(rows):
        return jnp.where(is_a, rows, before(rows))

    def theirs_before(rows):
        return jnp.where(is_a, before(rows), rows)

    def theirs_after(rows):
        return jnp.where(is_a, rows, after(rows))

    def fill_rim(a, rows):
        for jt in range(RUNS):
            rim = to_group(rows, jt, 0)
            xt[a, jt, OFF - 2 : OFF, :] = jnp.where(group == 0, rim, xt[a, jt, OFF - 2 : OFF, :])

    many = 8

    def block_ends(k, signal, reverse):
        def some(at, carry):
            jt = at // (MODES // many)
            first = lax.rem(at, MODES // many) * many
            lams = [lam[first + i] for i in range(many)]
            state = [None] * many
            for p in reversed(range(steps)) if reverse else range(steps):
                x = signal[jt, p]
                for i in range(many):
                    state[i] = x if state[i] is None else lams[i] * state[i] + x
            for i in range(many):
                pers = jnp.broadcast_to(par[3, pl.ds(first + i, 1), :], (SUB, 128))
                s = state[i]
                for d in sub_spans:
                    factor = jnp.exp(pers * (-1.0 * steps * d))
                    if reverse:
                        moved = jnp.where(sub_row < SUB - d, pltpu.roll(s, SUB - d, 0), 0.0)
                    else:
                        moved = jnp.where(sub_row >= d, pltpu.roll(s, d, 0), 0.0)
                    s = s + factor * moved
                if reverse:
                    ins[k, jt, first + i] = jnp.where(
                        sub_row < SUB - 1, pltpu.roll(s, SUB - 1, 0), 0.0
                    )
                    tots[k, jt, pl.ds(first + i, 1), :] = s[0:1, :]
                else:
                    ins[k, jt, first + i] = jnp.where(sub_row >= 1, pltpu.roll(s, 1, 0), 0.0)
                    tots[k, jt, pl.ds(first + i, 1), :] = s[SUB - 1 : SUB, :]
            return carry

        lax.fori_loop(0, RUNS * (MODES // many), some, 0)

    def run_ends(k, reverse):
        tiles = []
        for jt in range(RUNS):
            s = tots[k, jt]
            for d in (1, 2):
                if reverse:
                    moved = jnp.where(group < WIDE - d, pltpu.roll(s, 128 - chans * d, 1), 0.0)
                else:
                    moved = jnp.where(group >= d, pltpu.roll(s, chans * d, 1), 0.0)
                s = s + power(local_len * d) * moved
            tiles.append(s)
            tots[k, jt] = after(s) if reverse else before(s)
        return packed(tiles, 0 if reverse else WIDE - 1)

    arrived(rx.at[pl.ds(0, HALF - 1), pl.ds(1, 2)], 0)
    turn((1, 2))

    def gate_kv(jt, carry):
        for p in range(steps):
            key, value = path(1, jt, p), path(2, jt, p)
            u = rounded(key * value)
            ks[jt, p] = key
            vs[jt, p] = value
            us[jt, p] = jnp.where(corner, 0.0, u) if p < 2 else u
        return carry

    lax.fori_loop(0, RUNS, gate_kv, 0)
    block_ends(0, us, False)
    my_f = run_ends(0, False)
    k_last, v_last = last_rows(1), last_rows(2)
    k_first, v_first = first_rows(1), first_rows(2)
    edge[0, 0:MODES, :] = my_f
    edge[0, MODES : MODES + 8, :] = jnp.concatenate([k_last, v_last, k_first, v_first], axis=0)
    remote(edge.at[0], edge_in.at[0], 4, partner).start()

    arrived(rx.at[pl.ds(0, HALF - 1), 0], 1)
    arrived(rx.at[pl.ds(0, HALF - 1), 3], 2)
    turn((0, 3))

    def gate_q(jt, carry):
        for p in range(steps):
            query = path(0, jt, p)
            g = rounded(xt[3, jt, pl.ds(OFF + p, SUB, stride=steps), :] * query)
            qs[jt, p] = query
            gs[jt, p] = jnp.where(corner, 0.0, g) if p < 2 else g
        return carry

    lax.fori_loop(0, RUNS, gate_q, 0)
    block_ends(1, gs, True)
    my_b = run_ends(1, True)
    q_last, q_first, c_first = last_rows(0), first_rows(0), first_rows(3)
    edge[1, 0:MODES, :] = my_b
    edge[1, MODES : MODES + 8, :] = jnp.concatenate(
        [q_last, q_first, c_first, jnp.zeros((2, 128), F32)], axis=0
    )
    remote(edge.at[1], edge_in.at[1], 5, partner).start()

    arrived(edge_in.at[0], 4)
    their_f = edge_in[0, 0:MODES, :]
    rows = edge_in[0, MODES : MODES + 8, :]
    tk_last, tv_last, tk_first, tv_first = rows[0:2], rows[2:4], rows[4:6], rows[6:8]
    fill_rim(1, theirs_before(tk_last))
    fill_rim(2, theirs_before(tv_last))

    def regate_kv(jt, carry):
        for p in range(2):
            key, value = path(1, jt, p), path(2, jt, p)
            ks[jt, p] = key
            vs[jt, p] = value
            us[jt, p] = rounded(key * value)
        return carry

    lax.fori_loop(0, RUNS, regate_kv, 0)
    my_k = edge_path(1, k_first, theirs_before(tk_last))
    my_v = edge_path(2, v_first, theirs_before(tv_last))
    their_k = edge_path(1, tk_first, mine_before(k_last))
    their_v = edge_path(2, tv_first, mine_before(v_last))
    my_u = [rounded(k * v) for k, v in zip(my_k, my_v)]
    their_u = [rounded(k * v) for k, v in zip(their_k, their_v)]
    late = (power(run_len - 1), power(run_len - 2))
    my_f = my_f + late[0] * my_u[0] + late[1] * my_u[1]
    their_f = their_f + late[0] * their_u[0] + late[1] * their_u[1]
    a_f, b_f = jnp.where(is_a, my_f, their_f), jnp.where(is_a, their_f, my_f)
    scan = run_span * a_f + b_f
    scan = scan + pair_span * before(scan)
    scan = scan + power(4 * run_len) * jnp.where(group >= 2, pltpu.roll(scan, 2 * chans, 1), 0.0)
    into_a = before(scan)
    carry_f = jnp.where(is_a, into_a, run_span * into_a + a_f)
    next_f = run_span * carry_f + my_f
    whole_f = carry_f + inv_lam * (my_u[0] + inv_lam * my_u[1])
    for jt in range(RUNS):
        tots[0, jt] = tots[0, jt] + up_span * repeated(whole_f, jt)
        ends[jt] = repeated(carry_f, jt)

    def in_state(k, jt, m):
        pers = jnp.broadcast_to(par[3, pl.ds(m, 1), :], (SUB, 128))
        into = jnp.broadcast_to(tots[k, jt, pl.ds(m, 1), :], (SUB, 128))
        away = (sub_row if k == 0 else SUB - 1 - sub_row).astype(F32)
        state = ins[k, jt, m] + jnp.exp(pers * (-1.0 * steps) * away) * into
        if k == 0:
            exact = jnp.broadcast_to(ends[jt, pl.ds(m, 1), :], (SUB, 128))
            state = jnp.where(corner, exact, state)
        return state

    def filtered_by_modes(k, signal, jt):
        def some(at, totals):
            totals = list(totals)
            first = at * many
            lams = [lam[first + i] for i in range(many)]
            coefs = [coef[first + i] for i in range(many)]
            state = [in_state(k, jt, first + i) for i in range(many)]
            for i in range(many):
                ins[k, jt, first + i] = state[i]
            for p in reversed(range(steps)) if k else range(steps):
                x = signal[jt, p]
                parts = []
                for i in range(many):
                    state[i] = lams[i] * state[i] + x
                    parts.append(coefs[i] * state[i])
                while len(parts) > 1:
                    parts = [parts[i] + parts[i + 1] for i in range(0, len(parts), 2)]
                totals[p] = totals[p] + parts[0]
            return tuple(totals)

        skip = wt[9]
        start = tuple(skip * signal[jt, p] for p in range(steps))
        return lax.fori_loop(0, MODES // many, some, start)

    def conv_tile(jt, carry):
        totals = filtered_by_modes(0, us, jt)
        for p in range(steps):
            cv[jt, p] = rounded(totals[p])
        return carry

    lax.fori_loop(0, RUNS, conv_tile, 0)

    arrived(edge_in.at[1], 5)
    their_b = edge_in[1, 0:MODES, :]
    rows = edge_in[1, MODES : MODES + 8, :]
    tq_last, tq_first, tc_first = rows[0:2], rows[2:4], rows[4:6]
    fill_rim(0, theirs_before(tq_last))

    def regate_q(jt, carry):
        for p in range(2):
            query = path(0, jt, p)
            qs[jt, p] = query
            gs[jt, p] = rounded(xt[3, jt, pl.ds(OFF + p, SUB, stride=steps), :] * query)
        return carry

    lax.fori_loop(0, RUNS, regate_q, 0)

    def output_tile(jt, carry):
        for p in range(steps):
            at = pl.ds(p, SUB, stride=steps)
            conv = cv[jt, p]
            ot[jt, at, :] = qs[jt, p] * conv
            gf[0, jt, at, :] = xt[3, jt, pl.ds(OFF + p, SUB, stride=steps), :] * conv
        so[pl.ds(WIDE * jt, WIDE), 0] = (
            ot[jt].T.astype(BF16).reshape(WIDE, 2, own, local_len)
        )
        return carry

    lax.fori_loop(0, RUNS, output_tile, 0)

    def send_out(slot, x, w, device):
        remote(so.at[slot, 0], out_ref.at[my_x, :, my_w], 6, device).start()

    each_peer(send_out)

    my_q = edge_path(0, q_first, theirs_before(tq_last))
    their_q = edge_path(0, tq_first, mine_before(q_last))
    my_g = [rounded(my_q[i] * c_first[i : i + 1]) for i in range(2)]
    their_g = [rounded(their_q[i] * tc_first[i : i + 1]) for i in range(2)]
    my_b = my_b + my_g[0] + lam_rows * my_g[1]
    their_b = their_b + their_g[0] + lam_rows * their_g[1]
    a_b, b_b = jnp.where(is_a, my_b, their_b), jnp.where(is_a, their_b, my_b)
    scan = a_b + run_span * b_b
    scan = scan + pair_span * after(scan)
    scan = scan + power(4 * run_len) * jnp.where(
        group < RUNS - 2, pltpu.roll(scan, 128 - 2 * chans, 1), 0.0
    )
    into_b = after(scan)
    carry_b = jnp.where(is_a, run_span * into_b + b_b, into_b)
    for jt in range(RUNS):
        tots[1, jt] = tots[1, jt] + down_span * repeated(carry_b, jt)

    next_u = [theirs_after(u) for u in their_u]
    next_g = [theirs_after(g) for g in their_g]
    state0 = lam_rows * next_f + next_u[0]
    state1 = lam_rows * state0 + next_u[1]
    back0 = carry_b
    back1 = inv_lam * (carry_b - next_g[0])
    beyond = [[], [], []]
    for i, (state, back) in enumerate(((state0, back0), (state1, back1))):
        conv = rounded(
            jnp.sum(coef_rows * state, axis=0, keepdims=True) + skip_row * next_u[i]
        )
        back = rounded(jnp.sum(coef_rows * back, axis=0, keepdims=True) + skip_row * next_g[i])
        beyond[0].append(theirs_after(tc_first[i : i + 1]) * conv)
        beyond[1].append(back * theirs_after(their_v[i]))
        beyond[2].append(back * theirs_after(their_k[i]))

    def gf_rim(a):
        rows = jnp.concatenate(beyond[a] + [jnp.zeros((6, 128), F32)], axis=0)
        for jt in range(RUNS):
            inner = pltpu.roll(gf[a, jt, 0:8, :], 128 - chans, 1)
            gf[a, jt, local_len : local_len + 8, :] = jnp.where(
                group == WIDE - 1, to_group(rows, jt, WIDE - 1), inner
            )

    def grad_path(a, jt):
        total = None
        for j in range(TAPS):
            w = jnp.broadcast_to(wt[TAPS * a + j][0:1, :], (local_len, 128))
            term = w * gf[a, jt, j : j + local_len, :]
            total = term if total is None else total + term
        so[pl.ds(WIDE * jt, WIDE), 1 + a] = (
            total.T.astype(BF16).reshape(WIDE, 2, own, local_len)
        )

    def grad_taps(a, jt):
        return [
            jnp.sum(
                gf[a, jt, 0:local_len, :] * xt[a, jt, OFF - j : OFF - j + local_len, :],
                axis=0,
                keepdims=True,
            )
            for j in range(TAPS)
        ]

    gf_rim(0)

    def grad_q_tile(jt, carry):
        grad_path(0, jt)
        return carry

    lax.fori_loop(0, RUNS, grad_q_tile, 0)

    def send_gq(slot, x, w, device):
        remote(so.at[slot, 1], gproj_ref.at[0, my_x, :, my_w], 7, device).start()

    each_peer(send_gq)

    def back_tile(jt, skip_total):
        totals = filtered_by_modes(1, gs, jt)
        for p in range(steps):
            at = pl.ds(p, SUB, stride=steps)
            back = rounded(totals[p])
            gf[1, jt, at, :] = back * vs[jt, p]
            gf[2, jt, at, :] = back * ks[jt, p]
            skip_total = skip_total + us[jt, p] * gs[jt, p]
        return skip_total

    skip_total = lax.fori_loop(0, RUNS, back_tile, jnp.zeros((SUB, 128), F32))
    gf_rim(1)
    gf_rim(2)

    def grad_kv_tile(jt, carry):
        grad_path(1, jt)
        grad_path(2, jt)
        return carry

    lax.fori_loop(0, RUNS, grad_kv_tile, 0)

    def send_gkv(slot, x, w, device):
        remote(
            so.at[slot, pl.ds(2, 2)], gproj_ref.at[pl.ds(1, 2), my_x, :, my_w], 8, device
        ).start()

    each_peer(send_gkv)
    keep_out = [
        pltpu.make_async_copy(so.at[my_slot, 0], out_ref.at[my_x, :, my_w], local_sem.at[0]),
        pltpu.make_async_copy(
            so.at[my_slot, pl.ds(1, 3)], gproj_ref.at[:, my_x, :, my_w], local_sem.at[1]
        ),
    ]
    for copy in keep_out:
        copy.start()

    def taps_tile(jt, carry):
        found = [part for a in range(3) for part in grad_taps(a, jt)]
        return tuple(c + f for c, f in zip(carry, found))

    found = lax.fori_loop(0, RUNS, taps_tile, tuple(jnp.zeros((1, 128), F32) for _ in range(9)))
    rows = jnp.concatenate(
        list(found)
        + [jnp.sum(skip_total, axis=0, keepdims=True), jnp.zeros((6, 128), F32)],
        axis=0,
    )
    my_short = group_sum(rows) * (1.0 / root)
    sums[0, 0:16, :] = my_short
    remote(sums.at[0, pl.ds(0, 16)], sums_in.at[0, pl.ds(0, 16)], 9, partner).start()

    pacc[...] = jnp.zeros_like(pacc)
    racc[...] = jnp.zeros_like(racc)
    pair = 2

    def mode_sums(at, carry):
        jt = at // (MODES // pair)
        first = lax.rem(at, MODES // pair) * pair
        lams = [lam[first + i] for i in range(pair)]
        behind = [[None] * steps + [ins[1, jt, first + i]] for i in range(pair)]
        for p in reversed(range(1, steps)):
            g = gs[jt, p]
            for i in range(pair):
                behind[i][p] = lams[i] * behind[i][p + 1] + g
        plain = [None] * pair
        ramped = [None] * pair
        state = [ins[0, jt, first + i] for i in range(pair)]
        for p in range(steps):
            u = us[jt, p]
            g = gs[jt, p]
            for i in range(pair):
                state[i] = lams[i] * state[i] + u
                flat = g * state[i]
                ramp = behind[i][p + 1] * state[i]
                plain[i] = flat if plain[i] is None else plain[i] + flat
                ramped[i] = ramp if ramped[i] is None else ramped[i] + ramp
        for i in range(pair):
            pacc[first + i] += plain[i]
            racc[first + i] += ramped[i]
        return carry

    lax.fori_loop(0, RUNS * (MODES // pair), mode_sums, 0)
    my_plain = group_sum(
        jnp.concatenate([jnp.sum(pacc[m], axis=0, keepdims=True) for m in range(MODES)], axis=0)
    )
    my_ramped = group_sum(
        jnp.concatenate([jnp.sum(racc[m], axis=0, keepdims=True) for m in range(MODES)], axis=0)
    )
    sums[1, 0:MODES, :] = my_plain
    sums[1, MODES : 2 * MODES, :] = my_ramped
    remote(sums.at[1], sums_in.at[1], 10, partner).start()

    arrived(sums_in.at[0, pl.ds(0, 16)], 9)
    short = my_short + sums_in[0, 0:16, :]
    odd = lax.rem(my_w, 2) == 1
    other = pltpu.roll(short, own, 1)
    low, high = jnp.where(odd, other, short), jnp.where(odd, short, other)
    place = lane // own
    shorts[...] = jnp.where(place == my_w, low, jnp.where(place == my_w + WIDE, high, 0.0))
    each_peer(
        lambda slot, x, w, device: remote(shorts, all_short.at[my_slot], 11, device).start()
    )
    all_short[my_slot] = shorts[...]
    gskip_ref[...] = jnp.where(is_a, short[9:10, 0:own], short[9:10, own : 2 * own])

    arrived(sums_in.at[1], 10)
    plain = my_plain + sums_in[1, 0:MODES, :]
    ramped = lam_rows * (my_ramped + sums_in[1, MODES : 2 * MODES, :])
    grad_res = scale * plain / root
    grad_dec = residue * (jnp.exp(-2.0 * per) / scale * plain - scale * ramped) / (length * root)
    par[0, 0:MODES, :] = grad_res
    par[1, 0:MODES, :] = grad_dec
    for k, ref in ((0, gres_ref), (1, gdec_ref)):
        turned = par[k].T
        ref[...] = jnp.where(is_a, turned[0:own, 0:MODES], turned[own : 2 * own, 0:MODES])

    arrived(all_short.at[pl.ds(0, HALF - 1)], 11)
    for jt in range(RUNS):
        total = all_short[WIDE * jt]
        for w in range(1, WIDE):
            total = total + all_short[WIDE * jt + w]
        for i in range(3):
            gshort_ref[i, :, 128 * jt : 128 * (jt + 1)] = total[TAPS * i : TAPS * (i + 1), :]

    for copy in keep_out:
        copy.wait()
    most = pl.ds(0, HALF - 1)
    arrived(so.at[most, 0], 6)
    arrived(so.at[most, 1], 7)
    arrived(so.at[most, pl.ds(2, 2)], 8)
    left(rx.at[most, pl.ds(1, 2)], 0)
    left(rx.at[most, 0], 1)
    left(rx.at[most, 3], 2)
    left(filt.at[pl.ds(0, 3)], 3)
    left(edge.at[0], 4)
    left(edge.at[1], 5)
    left(so.at[most, 0], 6)
    left(so.at[most, 1], 7)
    left(so.at[most, pl.ds(2, 2)], 8)
    left(sums.at[0, pl.ds(0, 16)], 9)
    left(sums.at[1], 10)
    left(all_short.at[most], 11)


def per_device(projected, short_weight, residues, decay_rates, skip_weight, cotangent):
    n = lax.axis_size("context")
    channels, local_len = cotangent.shape
    own = channels // n
    steps = local_len // SUB
    vmem = pl.BlockSpec(memory_space=pltpu.VMEM)
    anywhere = pl.BlockSpec(memory_space=pl.ANY)
    stepped = pltpu.VMEM((RUNS, steps, SUB, 128), F32)
    blocks = (RUNS, 2, WIDE, own, local_len)
    results = pl.pallas_call(
        functools.partial(kernel, n, local_len, own),
        out_shape=(
            jax.ShapeDtypeStruct(blocks, BF16),
            jax.ShapeDtypeStruct((3,) + blocks, BF16),
            jax.ShapeDtypeStruct((3, TAPS, channels), F32),
            jax.ShapeDtypeStruct((own, MODES), F32),
            jax.ShapeDtypeStruct((own, MODES), F32),
            jax.ShapeDtypeStruct((1, own), F32),
        ),
        in_specs=[anywhere] * 6,
        out_specs=(anywhere, anywhere, vmem, vmem, vmem, vmem),
        scratch_shapes=[
            pltpu.VMEM((HALF, 4, 2, own, local_len), BF16),
            pltpu.VMEM((HALF, 4, 2, own, local_len), BF16),
            pltpu.VMEM((4, RUNS, OFF + local_len, 128), F32),
            stepped,
            stepped,
            stepped,
            stepped,
            stepped,
            stepped,
            pltpu.VMEM((3, RUNS, local_len + 8, 128), F32),
            pltpu.VMEM((RUNS, local_len, 128), F32),
            pltpu.VMEM((3, TAPS, channels), F32),
            pltpu.VMEM((6, own, MODES), F32),
            pltpu.VMEM((4, 128, 128), F32),
            pltpu.VMEM((10, SUB, 128), F32),
            pltpu.VMEM((MODES, SUB, 128), F32),
            pltpu.VMEM((MODES, SUB, 128), F32),
            pltpu.VMEM((2, RUNS, MODES, 128), F32),
            pltpu.VMEM((2, RUNS, MODES, SUB, 128), F32),
            pltpu.VMEM((RUNS, MODES, 128), F32),
            pltpu.VMEM((2, MODES + 8, 128), F32),
            pltpu.VMEM((2, MODES + 8, 128), F32),
            pltpu.VMEM((2, 2 * MODES, 128), F32),
            pltpu.VMEM((2, 2 * MODES, 128), F32),
            pltpu.VMEM((16, 128), F32),
            pltpu.VMEM((HALF, 16, 128), F32),
            pltpu.VMEM((MODES, SUB, 128), F32),
            pltpu.VMEM((MODES, SUB, 128), F32),
            pltpu.SemaphoreType.DMA((12,)),
            pltpu.SemaphoreType.DMA((12,)),
            pltpu.SemaphoreType.DMA((6,)),
        ],
        compiler_params=pltpu.CompilerParams(
            collective_id=0, has_side_effects=True, vmem_limit_bytes=56 * 1024 * 1024
        ),
    )(
        projected.reshape((3,) + blocks),
        cotangent.reshape(blocks),
        short_weight.transpose(0, 2, 1),
        decay_rates,
        residues,
        skip_weight.reshape(1, -1),
    )
    output, grad_projected, grad_short, grad_res, grad_dec, grad_skip = results
    return (
        output.reshape(channels, local_len),
        grad_projected.reshape(3, channels, local_len),
        grad_short.transpose(0, 2, 1),
        grad_res,
        grad_dec,
        grad_skip.reshape(-1),
    )


def solution(mesh):
    return jax.shard_map(
        per_device,
        mesh=mesh,
        in_specs=(
            P(None, "tensor", "context"),
            P(None, "tensor", None),
            P(("tensor", "context"), None),
            P(("tensor", "context"), None),
            P(("tensor", "context")),
            P("tensor", "context"),
        ),
        out_specs=(
            P("tensor", "context"),
            P(None, "tensor", "context"),
            P(None, "tensor", None),
            P(("tensor", "context"), None),
            P(("tensor", "context"), None),
            P(("tensor", "context")),
        ),
        check_vma=False,
    )
```

```python
import functools
import math

import jax
import jax.numpy as jnp
from jax import lax
from jax.experimental import pallas as pl
from jax.experimental.pallas import tpu as pltpu
from jax.sharding import PartitionSpec as P

MESH = pl.DeviceIdType.MESH
SUB = 8
MODES = 16
TAPS = 3
RIM = TAPS - 1
RUNS = 4
WIDE = 4
HALF = RUNS * WIDE
F32 = jnp.float32
BF16 = jnp.bfloat16


def rounded(value):
    return value.astype(BF16).astype(F32)


def one_minus_exp(x):
    series = jnp.ones_like(x)
    for k in range(10, 1, -1):
        series = 1.0 - x * (1.0 / k) * series
    return jnp.where(x < 0.5, x * series, 1.0 - jnp.exp(-x))


def kernel(
    n,
    local_len,
    own,
    proj_ref,
    cot_ref,
    sw_hbm,
    decay_hbm,
    res_hbm,
    skip_hbm,
    out_ref,
    gshort_ref,
    gres_ref,
    gdec_ref,
    gskip_ref,
    rx,
    so,
    xt,
    qs,
    ks,
    vs,
    us,
    gs,
    cv,
    gf,
    kept,
    sw,
    filt,
    par,
    wt,
    lam,
    coef,
    tots,
    ins,
    ends,
    edge,
    edge_in,
    sums,
    sums_in,
    shorts,
    all_short,
    pacc,
    racc,
    send_sem,
    recv_sem,
    local_sem,
):
    me = lax.axis_index("context")
    length = n * local_len
    steps = local_len // SUB
    chans = 2 * own
    root = math.sqrt(length)
    run_len = WIDE * local_len
    side = lax.rem(me // WIDE, 2)
    my_x = me // (2 * WIDE)
    my_w = lax.rem(me, WIDE)
    my_slot = my_x * WIDE + my_w
    partner = me + WIDE * (1 - 2 * side)
    is_a = side == 0

    def each_peer(body):
        def step(t, carry):
            slot = lax.rem(my_slot + t, HALF)
            x, w = slot // WIDE, lax.rem(slot, WIDE)
            body(slot, x, w, (2 * x + side) * WIDE + w)
            return carry

        lax.fori_loop(1, HALF, step, 0)

    def remote(src, dst, k, device):
        return pltpu.make_async_remote_copy(
            src_ref=src,
            dst_ref=dst,
            send_sem=send_sem.at[k],
            recv_sem=recv_sem.at[k],
            device_id={"context": device},
            device_id_type=MESH,
        )

    def arrived(ref, k):
        pltpu.make_async_copy(ref, ref, recv_sem.at[k]).wait()

    def left(ref, k):
        pltpu.make_async_copy(ref, ref, send_sem.at[k]).wait()

    barrier = pltpu.get_barrier_semaphore()
    pl.semaphore_signal(barrier, inc=1, device_id={"context": partner}, device_id_type=MESH)
    each_peer(
        lambda slot, x, w, device: pl.semaphore_signal(
            barrier, inc=1, device_id={"context": device}, device_id_type=MESH
        )
    )
    small = [
        pltpu.make_async_copy(sw_hbm, sw, local_sem.at[0]),
        pltpu.make_async_copy(decay_hbm, filt.at[0], local_sem.at[1]),
        pltpu.make_async_copy(res_hbm, filt.at[1], local_sem.at[2]),
        pltpu.make_async_copy(skip_hbm, filt.at[2, pl.ds(0, 1)], local_sem.at[3]),
    ]
    keep = [
        pltpu.make_async_copy(
            proj_ref.at[:, my_x, :, my_w], rx.at[my_slot, pl.ds(0, 3)], local_sem.at[4]
        ),
        pltpu.make_async_copy(cot_ref.at[my_x, :, my_w], rx.at[my_slot, 3], local_sem.at[5]),
    ]
    for copy in small + keep:
        copy.start()

    lane = lax.broadcasted_iota(jnp.int32, (1, 128), 1)
    group = lane // chans
    sub_row = lax.broadcasted_iota(jnp.int32, (SUB, 128), 0)
    corner = jnp.logical_and(sub_row == 0, group == 0)

    def group_sum(rows):
        width = chans
        while width < 128:
            rows = rows + pltpu.roll(rows, width, 1)
            width *= 2
        return rows

    def to_group(rows, here, there):
        shift = ((there - here) * chans) % 128
        return pltpu.roll(rows, shift, 1) if shift else rows

    def packed(tiles, here):
        total = None
        for jt in range(RUNS):
            piece = jnp.where(group == jt, to_group(tiles[jt], here, jt), 0.0)
            total = piece if total is None else total + piece
        return total

    def repeated(rows, jt):
        return group_sum(jnp.where(group == jt, rows, 0.0))

    def before(rows):
        return jnp.where(group >= 1, pltpu.roll(rows, chans, 1), 0.0)

    def after(rows):
        return jnp.where(group < RUNS - 1, pltpu.roll(rows, 128 - chans, 1), 0.0)

    for copy in small:
        copy.wait()
    pl.semaphore_wait(barrier, HALF)

    remote(filt.at[pl.ds(0, 3)], filt.at[pl.ds(3, 3)], 3, partner).start()

    def send_kv(slot, x, w, device):
        remote(proj_ref.at[pl.ds(1, 2), x, :, w], rx.at[my_slot, pl.ds(1, 2)], 0, device).start()

    def send_q_cot(slot, x, w, device):
        remote(proj_ref.at[0, x, :, w], rx.at[my_slot, 0], 1, device).start()
        remote(cot_ref.at[x, :, w], rx.at[my_slot, 3], 2, device).start()

    each_peer(send_kv)
    each_peer(send_q_cot)

    for i in range(3):
        rows = jnp.concatenate(
            [
                sw[i, :, pl.ds(pl.multiple_of(my_x * 128, 128), 128)],
                jnp.zeros((SUB - TAPS, 128), F32),
            ],
            axis=0,
        )
        rows = pltpu.roll(rows, lax.rem(128 - my_w * own, 128), 1)
        rows = jnp.where(lane < own, rows, 0.0) + pltpu.roll(
            jnp.where(jnp.logical_and(lane >= 64, lane < 64 + own), rows, 0.0), 64 + own, 1
        )
        rows = group_sum(rows)
        for j in range(TAPS):
            wt[TAPS * i + j] = jnp.broadcast_to(rows[j : j + 1, :], (SUB, 128))
    for copy in keep:
        copy.wait()
    arrived(filt.at[pl.ds(3, 3)], 3)
    par[...] = jnp.zeros_like(par)
    for k in range(2):
        mine, theirs = filt[k], filt[3 + k]
        first, second = jnp.where(is_a, mine, theirs), jnp.where(is_a, theirs, mine)
        for g in range(128 // chans):
            par[k, g * chans : g * chans + own, 0:MODES] = first
            par[k, g * chans + own : (g + 1) * chans, 0:MODES] = second
    mine, theirs = filt[2, 0:1, :], filt[5, 0:1, :]
    par[2, 0:1, 0:own] = jnp.where(is_a, mine, theirs)
    par[2, 1:2, 0:own] = jnp.where(is_a, theirs, mine)
    skip_row = group_sum(par[2, 0:1, :] + pltpu.roll(par[2, 1:2, :], own, 1))
    wt[9] = jnp.broadcast_to(skip_row, (SUB, 128))
    per = par[0].T[0:MODES, :] * (1.0 / length)
    residue = par[1].T[0:MODES, :]
    scale = jnp.sqrt(one_minus_exp(2.0 * per))
    coef_rows = residue * scale
    lam_rows = jnp.exp(-per)
    inv_lam = jnp.exp(per)
    par[3, 0:MODES, :] = per
    for m in range(MODES):
        lam[m] = jnp.broadcast_to(lam_rows[m : m + 1, :], (SUB, 128))
        coef[m] = jnp.broadcast_to(coef_rows[m : m + 1, :], (SUB, 128))

    def power(span):
        return jnp.exp(per * (-1.0 * span))

    sub_spans = [1, 2, 4]
    run_span, pair_span = power(run_len), power(2 * run_len)
    up_span = jnp.exp(per * (-1.0 * local_len) * group.astype(F32))
    down_span = jnp.exp(per * (-1.0 * local_len) * (WIDE - 1 - group).astype(F32))

    row = lax.broadcasted_iota(jnp.int32, (local_len, local_len), 0)
    column = lax.broadcasted_iota(jnp.int32, (local_len, local_len), 1)
    order = jnp.where(column == lax.rem(row, SUB) * steps + row // SUB, 1.0, 0.0).astype(BF16)

    def turn(arrays):
        def tile(jt, carry):
            for a in arrays:
                block = rx[pl.ds(WIDE * jt, WIDE), a].reshape(128, local_len)
                rows = lax.dot_general(
                    order, block, (((1,), (1,)), ((), ())), preferred_element_type=F32
                ).reshape(steps, SUB, 128)
                xt[a, jt, RIM : RIM + steps] = rows
                if a < 3:
                    for i in range(RIM):
                        moved = pltpu.roll(rows[steps - RIM + i], 1, 0)
                        first = jnp.where(group == 0, 0.0, pltpu.roll(moved, chans, 1))
                        xt[a, jt, i] = jnp.where(sub_row == 0, first, moved)
            return carry

        lax.fori_loop(0, RUNS, tile, 0)

    def turn_back(rows):
        flat = rows.astype(BF16).reshape(local_len, 128)
        return (
            lax.dot_general(flat, order, (((0,), (0,)), ((), ())), preferred_element_type=F32)
            .astype(BF16)
            .reshape(WIDE, 2, own, local_len)
        )

    def path(a, jt, p):
        total = None
        for j in range(TAPS):
            term = wt[TAPS * a + j] * xt[a, jt, RIM + p - j]
            total = term if total is None else total + term
        return total

    def last_rows(a):
        return packed(
            [
                jnp.concatenate(
                    [xt[a, jt, steps + i, SUB - 1 : SUB, :] for i in range(RIM)], axis=0
                )
                for jt in range(RUNS)
            ],
            WIDE - 1,
        )

    def first_rows(a):
        return packed(
            [
                jnp.concatenate([xt[a, jt, RIM + i, 0:1, :] for i in range(RIM)], axis=0)
                for jt in range(RUNS)
            ],
            0,
        )

    def edge_path(a, first, last):
        w = [wt[TAPS * a + j][0:1, :] for j in range(TAPS)]
        return (
            w[0] * first[0:1] + w[1] * last[1:2] + w[2] * last[0:1],
            w[0] * first[1:2] + w[1] * first[0:1] + w[2] * last[1:2],
        )

    def mine_before(rows):
        return jnp.where(is_a, rows, before(rows))

    def theirs_before(rows):
        return jnp.where(is_a, before(rows), rows)

    def theirs_after(rows):
        return jnp.where(is_a, rows, after(rows))

    def fill_rim(a, rows):
        for jt in range(RUNS):
            rim = to_group(rows, jt, 0)
            for i in range(RIM):
                xt[a, jt, i] = jnp.where(
                    corner, jnp.broadcast_to(rim[i : i + 1, :], (SUB, 128)), xt[a, jt, i]
                )

    many = 8

    def block_ends(k, signal, reverse):
        def some(at, carry):
            jt = at // (MODES // many)
            first = lax.rem(at, MODES // many) * many
            lams = [lam[first + i] for i in range(many)]
            state = [None] * many
            for p in reversed(range(steps)) if reverse else range(steps):
                x = signal[jt, p]
                for i in range(many):
                    state[i] = x if state[i] is None else lams[i] * state[i] + x
            for i in range(many):
                pers = jnp.broadcast_to(par[3, pl.ds(first + i, 1), :], (SUB, 128))
                s = state[i]
                for d in sub_spans:
                    factor = jnp.exp(pers * (-1.0 * steps * d))
                    if reverse:
                        moved = jnp.where(sub_row < SUB - d, pltpu.roll(s, SUB - d, 0), 0.0)
                    else:
                        moved = jnp.where(sub_row >= d, pltpu.roll(s, d, 0), 0.0)
                    s = s + factor * moved
                if reverse:
                    ins[k, jt, first + i] = jnp.where(
                        sub_row < SUB - 1, pltpu.roll(s, SUB - 1, 0), 0.0
                    )
                    tots[k, jt, pl.ds(first + i, 1), :] = s[0:1, :]
                else:
                    ins[k, jt, first + i] = jnp.where(sub_row >= 1, pltpu.roll(s, 1, 0), 0.0)
                    tots[k, jt, pl.ds(first + i, 1), :] = s[SUB - 1 : SUB, :]
            return carry

        lax.fori_loop(0, RUNS * (MODES // many), some, 0)

    def run_ends(k, reverse):
        tiles = []
        for jt in range(RUNS):
            s = tots[k, jt]
            for d in (1, 2):
                if reverse:
                    moved = jnp.where(group < WIDE - d, pltpu.roll(s, 128 - chans * d, 1), 0.0)
                else:
                    moved = jnp.where(group >= d, pltpu.roll(s, chans * d, 1), 0.0)
                s = s + power(local_len * d) * moved
            tiles.append(s)
            tots[k, jt] = after(s) if reverse else before(s)
        return packed(tiles, 0 if reverse else WIDE - 1)

    arrived(rx.at[pl.ds(0, HALF - 1), pl.ds(1, 2)], 0)
    turn((1, 2))

    def gate_kv(jt, carry):
        for p in range(steps):
            key, value = path(1, jt, p), path(2, jt, p)
            u = rounded(key * value)
            ks[jt, p] = key
            vs[jt, p] = value
            us[jt, p] = jnp.where(corner, 0.0, u) if p < 2 else u
        return carry

    lax.fori_loop(0, RUNS, gate_kv, 0)
    block_ends(0, us, False)
    my_f = run_ends(0, False)
    k_last, v_last = last_rows(1), last_rows(2)
    k_first, v_first = first_rows(1), first_rows(2)
    edge[0, 0:MODES, :] = my_f
    edge[0, MODES : MODES + 8, :] = jnp.concatenate([k_last, v_last, k_first, v_first], axis=0)
    remote(edge.at[0], edge_in.at[0], 4, partner).start()

    arrived(rx.at[pl.ds(0, HALF - 1), 0], 1)
    arrived(rx.at[pl.ds(0, HALF - 1), 3], 2)
    turn((0, 3))

    def gate_q(jt, carry):
        for p in range(steps):
            query = path(0, jt, p)
            g = rounded(xt[3, jt, RIM + p] * query)
            qs[jt, p] = query
            gs[jt, p] = jnp.where(corner, 0.0, g) if p < 2 else g
        return carry

    q_last, q_first, c_first = last_rows(0), first_rows(0), first_rows(3)
    edge[1, MODES : MODES + 8, :] = jnp.concatenate(
        [q_last, q_first, c_first, jnp.zeros((2, 128), F32)], axis=0
    )
    remote(
        edge.at[1, pl.ds(MODES, 8)], edge_in.at[1, pl.ds(MODES, 8)], 10, partner
    ).start()
    lax.fori_loop(0, RUNS, gate_q, 0)
    block_ends(1, gs, True)
    my_b = run_ends(1, True)
    edge[1, 0:MODES, :] = my_b
    remote(edge.at[1, pl.ds(0, MODES)], edge_in.at[1, pl.ds(0, MODES)], 5, partner).start()

    arrived(edge_in.at[0], 4)
    their_f = edge_in[0, 0:MODES, :]
    rows = edge_in[0, MODES : MODES + 8, :]
    tk_last, tv_last, tk_first, tv_first = rows[0:2], rows[2:4], rows[4:6], rows[6:8]
    fill_rim(1, theirs_before(tk_last))
    fill_rim(2, theirs_before(tv_last))

    def regate_kv(jt, carry):
        for p in range(2):
            key, value = path(1, jt, p), path(2, jt, p)
            ks[jt, p] = key
            vs[jt, p] = value
            us[jt, p] = rounded(key * value)
        return carry

    lax.fori_loop(0, RUNS, regate_kv, 0)
    my_k = edge_path(1, k_first, theirs_before(tk_last))
    my_v = edge_path(2, v_first, theirs_before(tv_last))
    their_k = edge_path(1, tk_first, mine_before(k_last))
    their_v = edge_path(2, tv_first, mine_before(v_last))
    my_u = [rounded(k * v) for k, v in zip(my_k, my_v)]
    their_u = [rounded(k * v) for k, v in zip(their_k, their_v)]
    late = (power(run_len - 1), power(run_len - 2))
    my_f = my_f + late[0] * my_u[0] + late[1] * my_u[1]
    their_f = their_f + late[0] * their_u[0] + late[1] * their_u[1]
    a_f, b_f = jnp.where(is_a, my_f, their_f), jnp.where(is_a, their_f, my_f)
    scan = run_span * a_f + b_f
    scan = scan + pair_span * before(scan)
    scan = scan + power(4 * run_len) * jnp.where(group >= 2, pltpu.roll(scan, 2 * chans, 1), 0.0)
    into_a = before(scan)
    carry_f = jnp.where(is_a, into_a, run_span * into_a + a_f)
    next_f = run_span * carry_f + my_f
    whole_f = carry_f + inv_lam * (my_u[0] + inv_lam * my_u[1])
    for jt in range(RUNS):
        tots[0, jt] = tots[0, jt] + up_span * repeated(whole_f, jt)
        ends[jt] = repeated(carry_f, jt)

    def in_state(k, jt, m):
        pers = jnp.broadcast_to(par[3, pl.ds(m, 1), :], (SUB, 128))
        into = jnp.broadcast_to(tots[k, jt, pl.ds(m, 1), :], (SUB, 128))
        away = (sub_row if k == 0 else SUB - 1 - sub_row).astype(F32)
        state = ins[k, jt, m] + jnp.exp(pers * (-1.0 * steps) * away) * into
        if k == 0:
            exact = jnp.broadcast_to(ends[jt, pl.ds(m, 1), :], (SUB, 128))
            state = jnp.where(corner, exact, state)
        return state

    def summed(parts):
        while len(parts) > 1:
            parts = [parts[i] + parts[i + 1] for i in range(0, len(parts), 2)]
        return parts[0]

    def conv_tile(jt, carry):
        def some(at, totals):
            totals = list(totals)
            first = at * many
            lams = [lam[first + i] for i in range(many)]
            coefs = [coef[first + i] for i in range(many)]
            state = [in_state(0, jt, first + i) for i in range(many)]
            for p in range(steps):
                u = us[jt, p]
                for i in range(many):
                    state[i] = lams[i] * state[i] + u
                    kept[jt, first + i, p] = state[i]
                totals[p] = totals[p] + summed([coefs[i] * state[i] for i in range(many)])
            return tuple(totals)

        start = tuple(wt[9] * us[jt, p] for p in range(steps))
        totals = lax.fori_loop(0, MODES // many, some, start)
        for p in range(steps):
            cv[jt, p] = rounded(totals[p])
        return carry

    lax.fori_loop(0, RUNS, conv_tile, 0)

    arrived(edge_in.at[1, pl.ds(MODES, 8)], 10)
    rows = edge_in[1, MODES : MODES + 8, :]
    tq_last, tq_first, tc_first = rows[0:2], rows[2:4], rows[4:6]
    fill_rim(0, theirs_before(tq_last))

    def regate_q(jt, carry):
        for p in range(2):
            query = path(0, jt, p)
            qs[jt, p] = query
            gs[jt, p] = rounded(xt[3, jt, RIM + p] * query)
        for p in range(steps):
            gf[0, jt, p] = xt[3, jt, RIM + p] * cv[jt, p]
        return carry

    lax.fori_loop(0, RUNS, regate_q, 0)
    next_u = [theirs_after(u) for u in their_u]
    next_c = theirs_after(tc_first)
    state0 = lam_rows * next_f + next_u[0]
    state1 = lam_rows * state0 + next_u[1]
    beyond = [[], [], []]
    for i, state in enumerate((state0, state1)):
        conv = rounded(
            jnp.sum(coef_rows * state, axis=0, keepdims=True) + skip_row * next_u[i]
        )
        beyond[0].append(next_c[i : i + 1] * conv)

    def gf_rim(a):
        for jt in range(RUNS):
            for i in range(RIM):
                rim = jnp.broadcast_to(to_group(beyond[a][i], jt, WIDE - 1), (SUB, 128))
                moved = pltpu.roll(gf[a, jt, i], SUB - 1, 0)
                last = jnp.where(group == WIDE - 1, rim, pltpu.roll(moved, 128 - chans, 1))
                gf[a, jt, steps + i] = jnp.where(sub_row == SUB - 1, last, moved)

    def grad_path(a, jt):
        w = [wt[TAPS * a + j] for j in range(TAPS)]
        rows = []
        for p in range(steps):
            total = w[0] * gf[a, jt, p]
            for j in range(1, TAPS):
                total = total + w[j] * gf[a, jt, p + j]
            rows.append(total)
        so[pl.ds(WIDE * jt, WIDE), 1 + a] = turn_back(jnp.stack(rows))

    def send_tile(jt, arrays, k):
        for w in range(WIDE):
            slot = WIDE * jt + w

            @pl.when(slot != my_slot)
            def _():
                remote(
                    so.at[slot, arrays],
                    out_ref.at[arrays, my_x, :, my_w],
                    k,
                    (2 * jt + side) * WIDE + w,
                ).start()

    gf_rim(0)

    def first_results(t, carry):
        jt = lax.rem(my_x + 1 + t, RUNS)
        so[pl.ds(WIDE * jt, WIDE), 0] = turn_back(
            jnp.stack([qs[jt, p] * cv[jt, p] for p in range(steps)])
        )
        grad_path(0, jt)
        send_tile(jt, pl.ds(0, 2), 7)
        return carry

    lax.fori_loop(0, RUNS, first_results, 0)

    my_q = edge_path(0, q_first, theirs_before(tq_last))
    their_q = edge_path(0, tq_first, mine_before(q_last))
    my_g = [rounded(my_q[i] * c_first[i : i + 1]) for i in range(2)]
    their_g = [rounded(their_q[i] * tc_first[i : i + 1]) for i in range(2)]
    arrived(edge_in.at[1, pl.ds(0, MODES)], 5)
    their_b = edge_in[1, 0:MODES, :]
    my_b = my_b + my_g[0] + lam_rows * my_g[1]
    their_b = their_b + their_g[0] + lam_rows * their_g[1]
    a_b, b_b = jnp.where(is_a, my_b, their_b), jnp.where(is_a, their_b, my_b)
    scan = a_b + run_span * b_b
    scan = scan + pair_span * after(scan)
    scan = scan + power(4 * run_len) * jnp.where(
        group < RUNS - 2, pltpu.roll(scan, 128 - 2 * chans, 1), 0.0
    )
    into_b = after(scan)
    carry_b = jnp.where(is_a, run_span * into_b + b_b, into_b)
    for jt in range(RUNS):
        tots[1, jt] = tots[1, jt] + down_span * repeated(carry_b, jt)

    next_g = [theirs_after(g) for g in their_g]
    for i, back in enumerate((carry_b, inv_lam * (carry_b - next_g[0]))):
        back = rounded(jnp.sum(coef_rows * back, axis=0, keepdims=True) + skip_row * next_g[i])
        beyond[1].append(back * theirs_after(their_v[i]))
        beyond[2].append(back * theirs_after(their_k[i]))

    def back_tile(jt, carry):
        def some(at, totals):
            totals = list(totals)
            first = at * many
            lams = [lam[first + i] for i in range(many)]
            coefs = [coef[first + i] for i in range(many)]
            state = [in_state(1, jt, first + i) for i in range(many)]
            for i in range(many):
                ins[1, jt, first + i] = state[i]
            for p in reversed(range(steps)):
                g = gs[jt, p]
                for i in range(many):
                    state[i] = lams[i] * state[i] + g
                totals[p] = totals[p] + summed([coefs[i] * state[i] for i in range(many)])
            return tuple(totals)

        carry = list(carry)
        start = tuple(wt[9] * gs[jt, p] for p in range(steps))
        totals = lax.fori_loop(0, MODES // many, some, start)
        for p in range(steps):
            back = rounded(totals[p])
            grads = (gf[0, jt, p], back * vs[jt, p], back * ks[jt, p])
            gf[1, jt, p] = grads[1]
            gf[2, jt, p] = grads[2]
            for a in range(3):
                for j in range(TAPS):
                    carry[TAPS * a + j] += grads[a] * xt[a, jt, RIM + p - j]
            carry[9] += us[jt, p] * gs[jt, p]
        return tuple(carry)

    found = lax.fori_loop(
        0, RUNS, back_tile, tuple(jnp.zeros((SUB, 128), F32) for _ in range(10))
    )

    rows = jnp.concatenate(
        [jnp.sum(part, axis=0, keepdims=True) for part in found] + [jnp.zeros((6, 128), F32)],
        axis=0,
    )
    my_short = group_sum(rows) * (1.0 / root)
    sums[0:16, :] = my_short
    remote(sums.at[pl.ds(0, 16)], sums_in.at[pl.ds(0, 16)], 6, partner).start()

    gf_rim(1)
    gf_rim(2)

    def last_results(t, carry):
        jt = lax.rem(my_x + 1 + t, RUNS)
        grad_path(1, jt)
        grad_path(2, jt)
        send_tile(jt, pl.ds(2, 2), 8)
        return carry

    lax.fori_loop(0, RUNS, last_results, 0)
    keep_out = pltpu.make_async_copy(so.at[my_slot], out_ref.at[:, my_x, :, my_w], local_sem.at[0])
    keep_out.start()

    pacc[...] = jnp.zeros_like(pacc)
    racc[...] = jnp.zeros_like(racc)
    few = 4

    def mode_sums(at, carry):
        jt = at // (MODES // few)
        first = lax.rem(at, MODES // few) * few
        lams = [lam[first + i] for i in range(few)]
        state = [ins[1, jt, first + i] for i in range(few)]
        plain = [None] * few
        ramped = [None] * few
        for p in reversed(range(steps)):
            g = gs[jt, p]
            for i in range(few):
                fwd = kept[jt, first + i, p]
                flat = g * fwd
                ramp = state[i] * fwd
                plain[i] = flat if plain[i] is None else plain[i] + flat
                ramped[i] = ramp if ramped[i] is None else ramped[i] + ramp
                state[i] = lams[i] * state[i] + g
        for i in range(few):
            pacc[first + i] += plain[i]
            racc[first + i] += ramped[i]
        return carry

    lax.fori_loop(0, RUNS * (MODES // few), mode_sums, 0)
    my_plain = group_sum(
        jnp.concatenate([jnp.sum(pacc[m], axis=0, keepdims=True) for m in range(MODES)], axis=0)
    )
    my_ramped = group_sum(
        jnp.concatenate([jnp.sum(racc[m], axis=0, keepdims=True) for m in range(MODES)], axis=0)
    )
    sums[16 : 16 + MODES, :] = my_plain
    sums[16 + MODES : 16 + 2 * MODES, :] = my_ramped
    remote(
        sums.at[pl.ds(16, 2 * MODES)], sums_in.at[pl.ds(16, 2 * MODES)], 11, partner
    ).start()

    arrived(sums_in.at[pl.ds(0, 16)], 6)
    short = my_short + sums_in[0:16, :]
    odd = lax.rem(my_w, 2) == 1
    other = pltpu.roll(short, own, 1)
    low = jnp.where(odd, other, short)[0:9, :]
    high = jnp.where(odd, short, other)[0:9, :]
    place = lane // own
    shorts[...] = jnp.where(place == my_w, low, jnp.where(place == my_w + WIDE, high, 0.0))
    each_peer(
        lambda slot, x, w, device: remote(shorts, all_short.at[my_slot], 9, device).start()
    )
    all_short[my_slot] = shorts[...]
    gskip_ref[...] = jnp.where(is_a, short[9:10, 0:own], short[9:10, own : 2 * own])

    arrived(sums_in.at[pl.ds(16, 2 * MODES)], 11)
    plain = my_plain + sums_in[16 : 16 + MODES, :]
    ramped = lam_rows * (my_ramped + sums_in[16 + MODES : 16 + 2 * MODES, :])
    grad_res = scale * plain / root
    grad_dec = residue * (jnp.exp(-2.0 * per) / scale * plain - scale * ramped) / (length * root)
    par[0, 0:MODES, :] = grad_res
    par[1, 0:MODES, :] = grad_dec
    for k, ref in ((0, gres_ref), (1, gdec_ref)):
        turned = par[k].T
        ref[...] = jnp.where(is_a, turned[0:own, 0:MODES], turned[own : 2 * own, 0:MODES])

    arrived(all_short.at[pl.ds(0, HALF - 1)], 9)
    for jt in range(RUNS):
        total = all_short[WIDE * jt]
        for w in range(1, WIDE):
            total = total + all_short[WIDE * jt + w]
        for i in range(3):
            gshort_ref[i, :, 128 * jt : 128 * (jt + 1)] = total[TAPS * i : TAPS * (i + 1), :]

    keep_out.wait()
    most = pl.ds(0, HALF - 1)
    arrived(so.at[most, pl.ds(0, 2)], 7)
    arrived(so.at[most, pl.ds(2, 2)], 8)
    left(rx.at[most, pl.ds(1, 2)], 0)
    left(rx.at[most, 0], 1)
    left(rx.at[most, 3], 2)
    left(filt.at[pl.ds(0, 3)], 3)
    left(edge.at[0], 4)
    left(edge.at[1, pl.ds(0, MODES)], 5)
    left(edge.at[1, pl.ds(MODES, 8)], 10)
    left(sums.at[pl.ds(0, 16)], 6)
    left(sums.at[pl.ds(16, 2 * MODES)], 11)
    left(so.at[most, pl.ds(0, 2)], 7)
    left(so.at[most, pl.ds(2, 2)], 8)
    left(all_short.at[most], 9)


def write_out(paths, short, res, dec, skip, out, gproj, gshort, gres, gdec, gskip):
    out[...] = paths[0]
    gproj[...] = paths[1:]
    gshort[...] = short[...]
    gres[...] = res[...]
    gdec[...] = dec[...]
    gskip[...] = skip[...]


def per_device(projected, short_weight, residues, decay_rates, skip_weight, cotangent):
    n = lax.axis_size("context")
    channels, local_len = cotangent.shape
    own = channels // n
    steps = local_len // SUB
    vmem = pl.BlockSpec(memory_space=pltpu.VMEM)
    hbm = pl.BlockSpec(memory_space=pltpu.HBM)
    stepped = pltpu.VMEM((RUNS, steps, SUB, 128), F32)
    blocks = (RUNS, 2, WIDE, own, local_len)
    small = (
        jax.ShapeDtypeStruct((3, TAPS, channels), F32),
        jax.ShapeDtypeStruct((own, MODES), F32),
        jax.ShapeDtypeStruct((own, MODES), F32),
        jax.ShapeDtypeStruct((1, own), F32),
    )
    results = pl.pallas_call(
        functools.partial(kernel, n, local_len, own),
        out_shape=(jax.ShapeDtypeStruct((4,) + blocks, BF16),) + small,
        in_specs=[hbm] * 6,
        out_specs=(vmem,) * 5,
        scratch_shapes=[
            pltpu.VMEM((HALF, 4, 2, own, local_len), BF16),
            pltpu.VMEM((HALF, 4, 2, own, local_len), BF16),
            pltpu.VMEM((4, RUNS, RIM + steps, SUB, 128), F32),
            stepped,
            stepped,
            stepped,
            stepped,
            stepped,
            stepped,
            pltpu.VMEM((3, RUNS, steps + RIM, SUB, 128), F32),
            pltpu.VMEM((RUNS, MODES, steps, SUB, 128), F32),
            pltpu.VMEM((3, TAPS, channels), F32),
            pltpu.VMEM((6, own, MODES), F32),
            pltpu.VMEM((4, 128, 128), F32),
            pltpu.VMEM((10, SUB, 128), F32),
            pltpu.VMEM((MODES, SUB, 128), F32),
            pltpu.VMEM((MODES, SUB, 128), F32),
            pltpu.VMEM((2, RUNS, MODES, 128), F32),
            pltpu.VMEM((2, RUNS, MODES, SUB, 128), F32),
            pltpu.VMEM((RUNS, MODES, 128), F32),
            pltpu.VMEM((2, MODES + 8, 128), F32),
            pltpu.VMEM((2, MODES + 8, 128), F32),
            pltpu.VMEM((16 + 2 * MODES, 128), F32),
            pltpu.VMEM((16 + 2 * MODES, 128), F32),
            pltpu.VMEM((9, 128), F32),
            pltpu.VMEM((HALF, 9, 128), F32),
            pltpu.VMEM((MODES, SUB, 128), F32),
            pltpu.VMEM((MODES, SUB, 128), F32),
            pltpu.SemaphoreType.DMA((12,)),
            pltpu.SemaphoreType.DMA((12,)),
            pltpu.SemaphoreType.DMA((6,)),
        ],
        compiler_params=pltpu.CompilerParams(
            collective_id=0, has_side_effects=True, vmem_limit_bytes=56 * 1024 * 1024
        ),
    )(
        projected.reshape((3,) + blocks),
        cotangent.reshape(blocks),
        short_weight.transpose(0, 2, 1),
        decay_rates,
        residues,
        skip_weight.reshape(1, -1),
    )
    output, grad_projected, grad_short, grad_res, grad_dec, grad_skip = pl.pallas_call(
        write_out,
        out_shape=(
            jax.ShapeDtypeStruct(blocks, BF16),
            jax.ShapeDtypeStruct((3,) + blocks, BF16),
        )
        + small,
        in_specs=[vmem] * 5,
        out_specs=(vmem,) * 6,
    )(*results)
    return (
        output.reshape(channels, local_len),
        grad_projected.reshape(3, channels, local_len),
        grad_short.transpose(0, 2, 1),
        grad_res,
        grad_dec,
        grad_skip.reshape(-1),
    )


def solution(mesh):
    return jax.shard_map(
        per_device,
        mesh=mesh,
        in_specs=(
            P(None, "tensor", "context"),
            P(None, "tensor", None),
            P(("tensor", "context"), None),
            P(("tensor", "context"), None),
            P(("tensor", "context")),
            P("tensor", "context"),
        ),
        out_specs=(
            P("tensor", "context"),
            P(None, "tensor", "context"),
            P(None, "tensor", None),
            P(("tensor", "context"), None),
            P(("tensor", "context"), None),
            P(("tensor", "context")),
        ),
        check_vma=False,
    )
```

```python
import functools
import math

import jax
import jax.numpy as jnp
from jax import lax
from jax.experimental import pallas as pl
from jax.experimental.pallas import tpu as pltpu
from jax.sharding import PartitionSpec as P

MESH = pl.DeviceIdType.MESH
SUB = 8
MODES = 16
TAPS = 3
RIM = TAPS - 1
RUNS = 4
WIDE = 4
HALF = RUNS * WIDE
F32 = jnp.float32
BF16 = jnp.bfloat16


def rounded(value):
    return value.astype(BF16).astype(F32)


def one_minus_exp(x):
    series = jnp.ones_like(x)
    for k in range(10, 1, -1):
        series = 1.0 - x * (1.0 / k) * series
    return jnp.where(x < 0.5, x * series, 1.0 - jnp.exp(-x))


def kernel(
    n,
    local_len,
    own,
    proj_ref,
    cot_ref,
    sw_hbm,
    decay_hbm,
    res_hbm,
    skip_hbm,
    land,
    all_short,
    gres_hbm,
    gdec_hbm,
    gskip_hbm,
    rx,
    so,
    xt,
    qs,
    ks,
    vs,
    us,
    gs,
    cv,
    gf,
    kept,
    sw,
    filt,
    par,
    wt,
    lam,
    coef,
    tots,
    ins,
    ends,
    edge,
    edge_in,
    sums,
    sums_in,
    shorts,
    gres,
    gskip,
    pacc,
    racc,
    send_sem,
    recv_sem,
    local_sem,
):
    me = lax.axis_index("context")
    length = n * local_len
    steps = local_len // SUB
    chans = 2 * own
    root = math.sqrt(length)
    run_len = WIDE * local_len
    side = lax.rem(me // WIDE, 2)
    my_x = me // (2 * WIDE)
    my_w = lax.rem(me, WIDE)
    my_slot = my_x * WIDE + my_w
    partner = me + WIDE * (1 - 2 * side)
    is_a = side == 0

    def each_peer(body):
        def step(t, carry):
            slot = lax.rem(my_slot + t, HALF)
            x, w = slot // WIDE, lax.rem(slot, WIDE)
            body(slot, x, w, (2 * x + side) * WIDE + w)
            return carry

        lax.fori_loop(1, HALF, step, 0)

    def remote(src, dst, k, device):
        return pltpu.make_async_remote_copy(
            src_ref=src,
            dst_ref=dst,
            send_sem=send_sem.at[k],
            recv_sem=recv_sem.at[k],
            device_id={"context": device},
            device_id_type=MESH,
        )

    def arrived(ref, k):
        pltpu.make_async_copy(ref, ref, recv_sem.at[k]).wait()

    def left(ref, k):
        pltpu.make_async_copy(ref, ref, send_sem.at[k]).wait()

    barrier = pltpu.get_barrier_semaphore()
    pl.semaphore_signal(barrier, inc=1, device_id={"context": partner}, device_id_type=MESH)
    each_peer(
        lambda slot, x, w, device: pl.semaphore_signal(
            barrier, inc=1, device_id={"context": device}, device_id_type=MESH
        )
    )
    small = [
        pltpu.make_async_copy(sw_hbm, sw, local_sem.at[0]),
        pltpu.make_async_copy(decay_hbm, filt.at[0], local_sem.at[1]),
        pltpu.make_async_copy(res_hbm, filt.at[1], local_sem.at[2]),
        pltpu.make_async_copy(skip_hbm, filt.at[2, pl.ds(0, 1)], local_sem.at[3]),
    ]
    keep = [
        pltpu.make_async_copy(
            proj_ref.at[:, my_x, :, my_w], rx.at[my_slot, pl.ds(0, 3)], local_sem.at[4]
        ),
        pltpu.make_async_copy(cot_ref.at[my_x, :, my_w], rx.at[my_slot, 3], local_sem.at[5]),
    ]
    for copy in small + keep:
        copy.start()

    lane = lax.broadcasted_iota(jnp.int32, (1, 128), 1)
    group = lane // chans
    sub_row = lax.broadcasted_iota(jnp.int32, (SUB, 128), 0)
    corner = jnp.logical_and(sub_row == 0, group == 0)

    def group_sum(rows):
        width = chans
        while width < 128:
            rows = rows + pltpu.roll(rows, width, 1)
            width *= 2
        return rows

    def to_group(rows, here, there):
        shift = ((there - here) * chans) % 128
        return pltpu.roll(rows, shift, 1) if shift else rows

    def packed(tiles, here):
        total = None
        for jt in range(RUNS):
            piece = jnp.where(group == jt, to_group(tiles[jt], here, jt), 0.0)
            total = piece if total is None else total + piece
        return total

    def repeated(rows, jt):
        return group_sum(jnp.where(group == jt, rows, 0.0))

    def before(rows):
        return jnp.where(group >= 1, pltpu.roll(rows, chans, 1), 0.0)

    def after(rows):
        return jnp.where(group < RUNS - 1, pltpu.roll(rows, 128 - chans, 1), 0.0)

    for copy in small:
        copy.wait()
    pl.semaphore_wait(barrier, HALF)

    remote(filt.at[pl.ds(0, 3)], filt.at[pl.ds(3, 3)], 3, partner).start()

    def send_kv(slot, x, w, device):
        remote(proj_ref.at[pl.ds(1, 2), x, :, w], rx.at[my_slot, pl.ds(1, 2)], 0, device).start()

    def send_q_cot(slot, x, w, device):
        remote(proj_ref.at[0, x, :, w], rx.at[my_slot, 0], 1, device).start()
        remote(cot_ref.at[x, :, w], rx.at[my_slot, 3], 2, device).start()

    each_peer(send_kv)
    each_peer(send_q_cot)

    for i in range(3):
        rows = jnp.concatenate(
            [
                sw[i, :, pl.ds(pl.multiple_of(my_x * 128, 128), 128)],
                jnp.zeros((SUB - TAPS, 128), F32),
            ],
            axis=0,
        )
        rows = pltpu.roll(rows, lax.rem(128 - my_w * own, 128), 1)
        rows = jnp.where(lane < own, rows, 0.0) + pltpu.roll(
            jnp.where(jnp.logical_and(lane >= 64, lane < 64 + own), rows, 0.0), 64 + own, 1
        )
        rows = group_sum(rows)
        for j in range(TAPS):
            wt[TAPS * i + j] = jnp.broadcast_to(rows[j : j + 1, :], (SUB, 128))
    for copy in keep:
        copy.wait()
    arrived(filt.at[pl.ds(3, 3)], 3)
    par[...] = jnp.zeros_like(par)
    for k in range(2):
        mine, theirs = filt[k], filt[3 + k]
        first, second = jnp.where(is_a, mine, theirs), jnp.where(is_a, theirs, mine)
        for g in range(128 // chans):
            par[k, g * chans : g * chans + own, 0:MODES] = first
            par[k, g * chans + own : (g + 1) * chans, 0:MODES] = second
    mine, theirs = filt[2, 0:1, :], filt[5, 0:1, :]
    par[2, 0:1, 0:own] = jnp.where(is_a, mine, theirs)
    par[2, 1:2, 0:own] = jnp.where(is_a, theirs, mine)
    skip_row = group_sum(par[2, 0:1, :] + pltpu.roll(par[2, 1:2, :], own, 1))
    wt[9] = jnp.broadcast_to(skip_row, (SUB, 128))
    per = par[0].T[0:MODES, :] * (1.0 / length)
    residue = par[1].T[0:MODES, :]
    scale = jnp.sqrt(one_minus_exp(2.0 * per))
    coef_rows = residue * scale
    lam_rows = jnp.exp(-per)
    inv_lam = jnp.exp(per)
    par[3, 0:MODES, :] = per
    for m in range(MODES):
        lam[m] = jnp.broadcast_to(lam_rows[m : m + 1, :], (SUB, 128))
        coef[m] = jnp.broadcast_to(coef_rows[m : m + 1, :], (SUB, 128))

    def power(span):
        return jnp.exp(per * (-1.0 * span))

    sub_spans = [1, 2, 4]
    run_span, pair_span = power(run_len), power(2 * run_len)
    up_span = jnp.exp(per * (-1.0 * local_len) * group.astype(F32))
    down_span = jnp.exp(per * (-1.0 * local_len) * (WIDE - 1 - group).astype(F32))

    row = lax.broadcasted_iota(jnp.int32, (local_len, local_len), 0)
    column = lax.broadcasted_iota(jnp.int32, (local_len, local_len), 1)
    order = jnp.where(column == lax.rem(row, SUB) * steps + row // SUB, 1.0, 0.0).astype(BF16)

    def turn(arrays):
        def tile(jt):
            for a in arrays:
                block = rx[pl.ds(WIDE * jt, WIDE), a].reshape(128, local_len)
                rows = lax.dot_general(
                    order, block, (((1,), (1,)), ((), ())), preferred_element_type=F32
                ).reshape(steps, SUB, 128)
                xt[a, jt, RIM : RIM + steps] = rows
                if a < 3:
                    for i in range(RIM):
                        moved = pltpu.roll(rows[steps - RIM + i], 1, 0)
                        first = jnp.where(group == 0, 0.0, pltpu.roll(moved, chans, 1))
                        xt[a, jt, i] = jnp.where(sub_row == 0, first, moved)

        for jt in range(RUNS):
            tile(jt)

    def turn_back(rows):
        flat = rows.astype(BF16).reshape(local_len, 128)
        return (
            lax.dot_general(flat, order, (((0,), (0,)), ((), ())), preferred_element_type=F32)
            .astype(BF16)
            .reshape(WIDE, 2, own, local_len)
        )

    def path(a, jt, p):
        total = None
        for j in range(TAPS):
            term = wt[TAPS * a + j] * xt[a, jt, RIM + p - j]
            total = term if total is None else total + term
        return total

    def last_rows(a):
        return packed(
            [
                jnp.concatenate(
                    [xt[a, jt, steps + i, SUB - 1 : SUB, :] for i in range(RIM)], axis=0
                )
                for jt in range(RUNS)
            ],
            WIDE - 1,
        )

    def first_rows(a):
        return packed(
            [
                jnp.concatenate([xt[a, jt, RIM + i, 0:1, :] for i in range(RIM)], axis=0)
                for jt in range(RUNS)
            ],
            0,
        )

    def edge_path(a, first, last):
        w = [wt[TAPS * a + j][0:1, :] for j in range(TAPS)]
        return (
            w[0] * first[0:1] + w[1] * last[1:2] + w[2] * last[0:1],
            w[0] * first[1:2] + w[1] * first[0:1] + w[2] * last[1:2],
        )

    def mine_before(rows):
        return jnp.where(is_a, rows, before(rows))

    def theirs_before(rows):
        return jnp.where(is_a, before(rows), rows)

    def theirs_after(rows):
        return jnp.where(is_a, rows, after(rows))

    def fill_rim(a, rows):
        for jt in range(RUNS):
            rim = to_group(rows, jt, 0)
            for i in range(RIM):
                xt[a, jt, i] = jnp.where(
                    corner, jnp.broadcast_to(rim[i : i + 1, :], (SUB, 128)), xt[a, jt, i]
                )

    many = 8

    def block_ends(k, signal, reverse):
        def some(at, carry):
            jt = at // (MODES // many)
            first = lax.rem(at, MODES // many) * many
            lams = [lam[first + i] for i in range(many)]
            state = [None] * many
            for p in reversed(range(steps)) if reverse else range(steps):
                x = signal[jt, p]
                for i in range(many):
                    state[i] = x if state[i] is None else lams[i] * state[i] + x
            for i in range(many):
                pers = jnp.broadcast_to(par[3, pl.ds(first + i, 1), :], (SUB, 128))
                s = state[i]
                for d in sub_spans:
                    factor = jnp.exp(pers * (-1.0 * steps * d))
                    if reverse:
                        moved = jnp.where(sub_row < SUB - d, pltpu.roll(s, SUB - d, 0), 0.0)
                    else:
                        moved = jnp.where(sub_row >= d, pltpu.roll(s, d, 0), 0.0)
                    s = s + factor * moved
                if reverse:
                    ins[k, jt, first + i] = jnp.where(
                        sub_row < SUB - 1, pltpu.roll(s, SUB - 1, 0), 0.0
                    )
                    tots[k, jt, pl.ds(first + i, 1), :] = s[0:1, :]
                else:
                    ins[k, jt, first + i] = jnp.where(sub_row >= 1, pltpu.roll(s, 1, 0), 0.0)
                    tots[k, jt, pl.ds(first + i, 1), :] = s[SUB - 1 : SUB, :]
            return carry

        lax.fori_loop(0, RUNS * (MODES // many), some, 0)

    def run_ends(k, reverse):
        tiles = []
        for jt in range(RUNS):
            s = tots[k, jt]
            for d in (1, 2):
                if reverse:
                    moved = jnp.where(group < WIDE - d, pltpu.roll(s, 128 - chans * d, 1), 0.0)
                else:
                    moved = jnp.where(group >= d, pltpu.roll(s, chans * d, 1), 0.0)
                s = s + power(local_len * d) * moved
            tiles.append(s)
            tots[k, jt] = after(s) if reverse else before(s)
        return packed(tiles, 0 if reverse else WIDE - 1)

    arrived(rx.at[pl.ds(0, HALF - 1), pl.ds(1, 2)], 0)
    turn((1, 2))

    def gate_kv(jt, carry):
        for p in range(steps):
            key, value = path(1, jt, p), path(2, jt, p)
            u = rounded(key * value)
            ks[jt, p] = key
            vs[jt, p] = value
            us[jt, p] = jnp.where(corner, 0.0, u) if p < 2 else u
        return carry

    lax.fori_loop(0, RUNS, gate_kv, 0)
    block_ends(0, us, False)
    my_f = run_ends(0, False)
    k_last, v_last = last_rows(1), last_rows(2)
    k_first, v_first = first_rows(1), first_rows(2)
    edge[0, 0:MODES, :] = my_f
    edge[0, MODES : MODES + 8, :] = jnp.concatenate([k_last, v_last, k_first, v_first], axis=0)
    remote(edge.at[0], edge_in.at[0], 4, partner).start()

    arrived(rx.at[pl.ds(0, HALF - 1), 0], 1)
    arrived(rx.at[pl.ds(0, HALF - 1), 3], 2)
    turn((0, 3))

    def gate_q(jt, carry):
        for p in range(steps):
            query = path(0, jt, p)
            g = rounded(xt[3, jt, RIM + p] * query)
            qs[jt, p] = query
            gs[jt, p] = jnp.where(corner, 0.0, g) if p < 2 else g
        return carry

    q_last, q_first, c_first = last_rows(0), first_rows(0), first_rows(3)
    edge[1, MODES : MODES + 8, :] = jnp.concatenate(
        [q_last, q_first, c_first, jnp.zeros((2, 128), F32)], axis=0
    )
    remote(
        edge.at[1, pl.ds(MODES, 8)], edge_in.at[1, pl.ds(MODES, 8)], 10, partner
    ).start()
    lax.fori_loop(0, RUNS, gate_q, 0)
    block_ends(1, gs, True)
    my_b = run_ends(1, True)
    edge[1, 0:MODES, :] = my_b
    remote(edge.at[1, pl.ds(0, MODES)], edge_in.at[1, pl.ds(0, MODES)], 5, partner).start()

    arrived(edge_in.at[0], 4)
    their_f = edge_in[0, 0:MODES, :]
    rows = edge_in[0, MODES : MODES + 8, :]
    tk_last, tv_last, tk_first, tv_first = rows[0:2], rows[2:4], rows[4:6], rows[6:8]
    fill_rim(1, theirs_before(tk_last))
    fill_rim(2, theirs_before(tv_last))

    def regate_kv(jt, carry):
        for p in range(2):
            key, value = path(1, jt, p), path(2, jt, p)
            ks[jt, p] = key
            vs[jt, p] = value
            us[jt, p] = rounded(key * value)
        return carry

    lax.fori_loop(0, RUNS, regate_kv, 0)
    my_k = edge_path(1, k_first, theirs_before(tk_last))
    my_v = edge_path(2, v_first, theirs_before(tv_last))
    their_k = edge_path(1, tk_first, mine_before(k_last))
    their_v = edge_path(2, tv_first, mine_before(v_last))
    my_u = [rounded(k * v) for k, v in zip(my_k, my_v)]
    their_u = [rounded(k * v) for k, v in zip(their_k, their_v)]
    late = (power(run_len - 1), power(run_len - 2))
    my_f = my_f + late[0] * my_u[0] + late[1] * my_u[1]
    their_f = their_f + late[0] * their_u[0] + late[1] * their_u[1]
    a_f, b_f = jnp.where(is_a, my_f, their_f), jnp.where(is_a, their_f, my_f)
    scan = run_span * a_f + b_f
    scan = scan + pair_span * before(scan)
    scan = scan + power(4 * run_len) * jnp.where(group >= 2, pltpu.roll(scan, 2 * chans, 1), 0.0)
    into_a = before(scan)
    carry_f = jnp.where(is_a, into_a, run_span * into_a + a_f)
    next_f = run_span * carry_f + my_f
    whole_f = carry_f + inv_lam * (my_u[0] + inv_lam * my_u[1])
    for jt in range(RUNS):
        tots[0, jt] = tots[0, jt] + up_span * repeated(whole_f, jt)
        ends[jt] = repeated(carry_f, jt)

    def in_state(k, jt, m):
        pers = jnp.broadcast_to(par[3, pl.ds(m, 1), :], (SUB, 128))
        into = jnp.broadcast_to(tots[k, jt, pl.ds(m, 1), :], (SUB, 128))
        away = (sub_row if k == 0 else SUB - 1 - sub_row).astype(F32)
        state = ins[k, jt, m] + jnp.exp(pers * (-1.0 * steps) * away) * into
        if k == 0:
            exact = jnp.broadcast_to(ends[jt, pl.ds(m, 1), :], (SUB, 128))
            state = jnp.where(corner, exact, state)
        return state

    def summed(parts):
        while len(parts) > 1:
            parts = [parts[i] + parts[i + 1] for i in range(0, len(parts), 2)]
        return parts[0]

    def conv_tile(jt, carry):
        def some(at, totals):
            totals = list(totals)
            first = at * many
            lams = [lam[first + i] for i in range(many)]
            coefs = [coef[first + i] for i in range(many)]
            state = [in_state(0, jt, first + i) for i in range(many)]
            for p in range(steps):
                u = us[jt, p]
                for i in range(many):
                    state[i] = lams[i] * state[i] + u
                    kept[jt, first + i, p] = state[i]
                totals[p] = totals[p] + summed([coefs[i] * state[i] for i in range(many)])
            return tuple(totals)

        start = tuple(wt[9] * us[jt, p] for p in range(steps))
        totals = lax.fori_loop(0, MODES // many, some, start)
        for p in range(steps):
            cv[jt, p] = rounded(totals[p])
        return carry

    lax.fori_loop(0, RUNS, conv_tile, 0)

    arrived(edge_in.at[1, pl.ds(MODES, 8)], 10)
    rows = edge_in[1, MODES : MODES + 8, :]
    tq_last, tq_first, tc_first = rows[0:2], rows[2:4], rows[4:6]
    fill_rim(0, theirs_before(tq_last))

    def regate_q(jt, carry):
        for p in range(2):
            query = path(0, jt, p)
            qs[jt, p] = query
            gs[jt, p] = rounded(xt[3, jt, RIM + p] * query)
        for p in range(steps):
            gf[0, jt, p] = xt[3, jt, RIM + p] * cv[jt, p]
        return carry

    lax.fori_loop(0, RUNS, regate_q, 0)
    next_u = [theirs_after(u) for u in their_u]
    next_c = theirs_after(tc_first)
    state0 = lam_rows * next_f + next_u[0]
    state1 = lam_rows * state0 + next_u[1]
    beyond = [[], [], []]
    for i, state in enumerate((state0, state1)):
        conv = rounded(
            jnp.sum(coef_rows * state, axis=0, keepdims=True) + skip_row * next_u[i]
        )
        beyond[0].append(next_c[i : i + 1] * conv)

    def gf_rim(a):
        for jt in range(RUNS):
            for i in range(RIM):
                rim = jnp.broadcast_to(to_group(beyond[a][i], jt, WIDE - 1), (SUB, 128))
                moved = pltpu.roll(gf[a, jt, i], SUB - 1, 0)
                last = jnp.where(group == WIDE - 1, rim, pltpu.roll(moved, 128 - chans, 1))
                gf[a, jt, steps + i] = jnp.where(sub_row == SUB - 1, last, moved)

    def grad_path(a, jt):
        w = [wt[TAPS * a + j] for j in range(TAPS)]
        rows = []
        for p in range(steps):
            total = w[0] * gf[a, jt, p]
            for j in range(1, TAPS):
                total = total + w[j] * gf[a, jt, p + j]
            rows.append(total)
        so[pl.ds(WIDE * jt, WIDE), 1 + a] = turn_back(jnp.stack(rows))

    def send_tile(jt, arrays, k):
        for w in range(WIDE):
            slot = WIDE * jt + w

            @pl.when(slot != my_slot)
            def _():
                remote(
                    so.at[slot, arrays],
                    land.at[my_slot, arrays],
                    k,
                    (2 * jt + side) * WIDE + w,
                ).start()

    gf_rim(0)

    def first_results(t, carry):
        jt = lax.rem(my_x + 1 + t, RUNS)
        so[pl.ds(WIDE * jt, WIDE), 0] = turn_back(
            jnp.stack([qs[jt, p] * cv[jt, p] for p in range(steps)])
        )
        grad_path(0, jt)
        send_tile(jt, pl.ds(0, 2), 7)
        return carry

    lax.fori_loop(0, RUNS, first_results, 0)

    my_q = edge_path(0, q_first, theirs_before(tq_last))
    their_q = edge_path(0, tq_first, mine_before(q_last))
    my_g = [rounded(my_q[i] * c_first[i : i + 1]) for i in range(2)]
    their_g = [rounded(their_q[i] * tc_first[i : i + 1]) for i in range(2)]
    arrived(edge_in.at[1, pl.ds(0, MODES)], 5)
    their_b = edge_in[1, 0:MODES, :]
    my_b = my_b + my_g[0] + lam_rows * my_g[1]
    their_b = their_b + their_g[0] + lam_rows * their_g[1]
    a_b, b_b = jnp.where(is_a, my_b, their_b), jnp.where(is_a, their_b, my_b)
    scan = a_b + run_span * b_b
    scan = scan + pair_span * after(scan)
    scan = scan + power(4 * run_len) * jnp.where(
        group < RUNS - 2, pltpu.roll(scan, 128 - 2 * chans, 1), 0.0
    )
    into_b = after(scan)
    carry_b = jnp.where(is_a, run_span * into_b + b_b, into_b)
    for jt in range(RUNS):
        tots[1, jt] = tots[1, jt] + down_span * repeated(carry_b, jt)

    next_g = [theirs_after(g) for g in their_g]
    for i, back in enumerate((carry_b, inv_lam * (carry_b - next_g[0]))):
        back = rounded(jnp.sum(coef_rows * back, axis=0, keepdims=True) + skip_row * next_g[i])
        beyond[1].append(back * theirs_after(their_v[i]))
        beyond[2].append(back * theirs_after(their_k[i]))

    def back_tile(jt, carry):
        def some(at, totals):
            totals = list(totals)
            first = at * many
            lams = [lam[first + i] for i in range(many)]
            coefs = [coef[first + i] for i in range(many)]
            state = [in_state(1, jt, first + i) for i in range(many)]
            for i in range(many):
                ins[1, jt, first + i] = state[i]
            for p in reversed(range(steps)):
                g = gs[jt, p]
                for i in range(many):
                    state[i] = lams[i] * state[i] + g
                totals[p] = totals[p] + summed([coefs[i] * state[i] for i in range(many)])
            return tuple(totals)

        carry = list(carry)
        start = tuple(wt[9] * gs[jt, p] for p in range(steps))
        totals = lax.fori_loop(0, MODES // many, some, start)
        for p in range(steps):
            back = rounded(totals[p])
            grads = (gf[0, jt, p], back * vs[jt, p], back * ks[jt, p])
            gf[1, jt, p] = grads[1]
            gf[2, jt, p] = grads[2]
            for a in range(3):
                for j in range(TAPS):
                    carry[TAPS * a + j] += grads[a] * xt[a, jt, RIM + p - j]
            carry[9] += us[jt, p] * gs[jt, p]
        return tuple(carry)

    found = lax.fori_loop(
        0, RUNS, back_tile, tuple(jnp.zeros((SUB, 128), F32) for _ in range(10))
    )

    rows = jnp.concatenate(
        [jnp.sum(part, axis=0, keepdims=True) for part in found] + [jnp.zeros((6, 128), F32)],
        axis=0,
    )
    my_short = group_sum(rows) * (1.0 / root)
    sums[0:16, :] = my_short
    remote(sums.at[pl.ds(0, 16)], sums_in.at[pl.ds(0, 16)], 6, partner).start()

    gf_rim(1)
    gf_rim(2)

    def last_results(t, carry):
        jt = lax.rem(my_x + 1 + t, RUNS)
        grad_path(1, jt)
        grad_path(2, jt)
        send_tile(jt, pl.ds(2, 2), 8)
        return carry

    lax.fori_loop(0, RUNS, last_results, 0)
    keep_out = [pltpu.make_async_copy(so.at[my_slot], land.at[my_slot], local_sem.at[0])]
    keep_out[0].start()

    pacc[...] = jnp.zeros_like(pacc)
    racc[...] = jnp.zeros_like(racc)
    few = 4

    def mode_sums(at, carry):
        jt = at // (MODES // few)
        first = lax.rem(at, MODES // few) * few
        lams = [lam[first + i] for i in range(few)]
        state = [ins[1, jt, first + i] for i in range(few)]
        plain = [None] * few
        ramped = [None] * few
        for p in reversed(range(steps)):
            g = gs[jt, p]
            for i in range(few):
                fwd = kept[jt, first + i, p]
                flat = g * fwd
                ramp = state[i] * fwd
                plain[i] = flat if plain[i] is None else plain[i] + flat
                ramped[i] = ramp if ramped[i] is None else ramped[i] + ramp
                state[i] = lams[i] * state[i] + g
        for i in range(few):
            pacc[first + i] += plain[i]
            racc[first + i] += ramped[i]
        return carry

    lax.fori_loop(0, RUNS * (MODES // few), mode_sums, 0)
    my_plain = group_sum(
        jnp.concatenate([jnp.sum(pacc[m], axis=0, keepdims=True) for m in range(MODES)], axis=0)
    )
    my_ramped = group_sum(
        jnp.concatenate([jnp.sum(racc[m], axis=0, keepdims=True) for m in range(MODES)], axis=0)
    )
    sums[16 : 16 + MODES, :] = my_plain
    sums[16 + MODES : 16 + 2 * MODES, :] = my_ramped
    remote(
        sums.at[pl.ds(16, 2 * MODES)], sums_in.at[pl.ds(16, 2 * MODES)], 11, partner
    ).start()

    arrived(sums_in.at[pl.ds(0, 16)], 6)
    short = my_short + sums_in[0:16, :]
    odd = lax.rem(my_w, 2) == 1
    other = pltpu.roll(short, own, 1)
    low = jnp.where(odd, other, short)[0:9, :]
    high = jnp.where(odd, short, other)[0:9, :]
    place = lane // own
    shorts[...] = jnp.where(place == my_w, low, jnp.where(place == my_w + WIDE, high, 0.0))
    each_peer(
        lambda slot, x, w, device: remote(shorts, all_short.at[my_slot], 9, device).start()
    )
    gskip[...] = jnp.where(is_a, short[9:10, 0:own], short[9:10, own : 2 * own])

    arrived(sums_in.at[pl.ds(16, 2 * MODES)], 11)
    plain = my_plain + sums_in[16 : 16 + MODES, :]
    ramped = lam_rows * (my_ramped + sums_in[16 + MODES : 16 + 2 * MODES, :])
    grad_res = scale * plain / root
    grad_dec = residue * (jnp.exp(-2.0 * per) / scale * plain - scale * ramped) / (length * root)
    par[0, 0:MODES, :] = grad_res
    par[1, 0:MODES, :] = grad_dec
    for k in range(2):
        turned = par[k].T
        gres[k] = jnp.where(is_a, turned[0:own, 0:MODES], turned[own : 2 * own, 0:MODES])
    for at, (src, dst) in enumerate(
        (
            (shorts, all_short.at[my_slot]),
            (gres.at[0], gres_hbm),
            (gres.at[1], gdec_hbm),
            (gskip, gskip_hbm),
        )
    ):
        keep_out.append(pltpu.make_async_copy(src, dst, local_sem.at[1 + at]))
        keep_out[-1].start()

    arrived(all_short.at[pl.ds(0, HALF - 1)], 9)
    for copy in keep_out:
        copy.wait()
    most = pl.ds(0, HALF - 1)
    arrived(so.at[most, pl.ds(0, 2)], 7)
    arrived(so.at[most, pl.ds(2, 2)], 8)
    left(rx.at[most, pl.ds(1, 2)], 0)
    left(rx.at[most, 0], 1)
    left(rx.at[most, 3], 2)
    left(filt.at[pl.ds(0, 3)], 3)
    left(edge.at[0], 4)
    left(edge.at[1, pl.ds(0, MODES)], 5)
    left(edge.at[1, pl.ds(MODES, 8)], 10)
    left(sums.at[pl.ds(0, 16)], 6)
    left(sums.at[pl.ds(16, 2 * MODES)], 11)
    left(so.at[most, pl.ds(0, 2)], 7)
    left(so.at[most, pl.ds(2, 2)], 8)
    left(all_short.at[most], 9)


def write_out(land, parts, res, dec, skip, out, gproj, gshort, gres, gdec, gskip):
    for x in range(RUNS):
        for half in range(2):
            for w in range(WIDE):
                out[x, half, w] = land[WIDE * x + w, 0, half]
                for a in range(3):
                    gproj[a, x, half, w] = land[WIDE * x + w, 1 + a, half]
        total = parts[WIDE * x]
        for w in range(1, WIDE):
            total = total + parts[WIDE * x + w]
        for i in range(3):
            gshort[i, :, 128 * x : 128 * (x + 1)] = total[TAPS * i : TAPS * (i + 1), :]
    gres[...] = res[...]
    gdec[...] = dec[...]
    gskip[...] = skip[...]


def per_device(projected, short_weight, residues, decay_rates, skip_weight, cotangent):
    n = lax.axis_size("context")
    channels, local_len = cotangent.shape
    own = channels // n
    steps = local_len // SUB
    vmem = pl.BlockSpec(memory_space=pltpu.VMEM)
    hbm = pl.BlockSpec(memory_space=pltpu.HBM)
    stepped = pltpu.VMEM((RUNS, steps, SUB, 128), F32)
    blocks = (RUNS, 2, WIDE, own, local_len)
    small = (
        jax.ShapeDtypeStruct((own, MODES), F32),
        jax.ShapeDtypeStruct((own, MODES), F32),
        jax.ShapeDtypeStruct((1, own), F32),
    )
    results = pl.pallas_call(
        functools.partial(kernel, n, local_len, own),
        out_shape=(
            jax.ShapeDtypeStruct((HALF, 4, 2, own, local_len), BF16),
            jax.ShapeDtypeStruct((HALF, 3 * TAPS, 128), F32),
        )
        + small,
        in_specs=[hbm] * 6,
        out_specs=(hbm,) * 5,
        scratch_shapes=[
            pltpu.VMEM((HALF, 4, 2, own, local_len), BF16),
            pltpu.VMEM((HALF, 4, 2, own, local_len), BF16),
            pltpu.VMEM((4, RUNS, RIM + steps, SUB, 128), F32),
            stepped,
            stepped,
            stepped,
            stepped,
            stepped,
            stepped,
            pltpu.VMEM((3, RUNS, steps + RIM, SUB, 128), F32),
            pltpu.VMEM((RUNS, MODES, steps, SUB, 128), F32),
            pltpu.VMEM((3, TAPS, channels), F32),
            pltpu.VMEM((6, own, MODES), F32),
            pltpu.VMEM((4, 128, 128), F32),
            pltpu.VMEM((10, SUB, 128), F32),
            pltpu.VMEM((MODES, SUB, 128), F32),
            pltpu.VMEM((MODES, SUB, 128), F32),
            pltpu.VMEM((2, RUNS, MODES, 128), F32),
            pltpu.VMEM((2, RUNS, MODES, SUB, 128), F32),
            pltpu.VMEM((RUNS, MODES, 128), F32),
            pltpu.VMEM((2, MODES + 8, 128), F32),
            pltpu.VMEM((2, MODES + 8, 128), F32),
            pltpu.VMEM((16 + 2 * MODES, 128), F32),
            pltpu.VMEM((16 + 2 * MODES, 128), F32),
            pltpu.VMEM((9, 128), F32),
            pltpu.VMEM((2, own, MODES), F32),
            pltpu.VMEM((1, own), F32),
            pltpu.VMEM((MODES, SUB, 128), F32),
            pltpu.VMEM((MODES, SUB, 128), F32),
            pltpu.SemaphoreType.DMA((12,)),
            pltpu.SemaphoreType.DMA((12,)),
            pltpu.SemaphoreType.DMA((6,)),
        ],
        compiler_params=pltpu.CompilerParams(
            collective_id=0, has_side_effects=True, vmem_limit_bytes=56 * 1024 * 1024
        ),
    )(
        projected.reshape((3,) + blocks),
        cotangent.reshape(blocks),
        short_weight.transpose(0, 2, 1),
        decay_rates,
        residues,
        skip_weight.reshape(1, -1),
    )
    output, grad_projected, grad_short, grad_res, grad_dec, grad_skip = pl.pallas_call(
        write_out,
        out_shape=(
            jax.ShapeDtypeStruct(blocks, BF16),
            jax.ShapeDtypeStruct((3,) + blocks, BF16),
            jax.ShapeDtypeStruct((3, TAPS, channels), F32),
        )
        + small,
        in_specs=[vmem] * 5,
        out_specs=(vmem,) * 6,
    )(*results)
    return (
        output.reshape(channels, local_len),
        grad_projected.reshape(3, channels, local_len),
        grad_short.transpose(0, 2, 1),
        grad_res,
        grad_dec,
        grad_skip.reshape(-1),
    )


def solution(mesh):
    return jax.shard_map(
        per_device,
        mesh=mesh,
        in_specs=(
            P(None, "tensor", "context"),
            P(None, "tensor", None),
            P(("tensor", "context"), None),
            P(("tensor", "context"), None),
            P(("tensor", "context")),
            P("tensor", "context"),
        ),
        out_specs=(
            P("tensor", "context"),
            P(None, "tensor", "context"),
            P(None, "tensor", None),
            P(("tensor", "context"), None),
            P(("tensor", "context"), None),
            P(("tensor", "context")),
        ),
        check_vma=False,
    )
```

```python
import functools
import math

import jax
import jax.numpy as jnp
from jax import lax
from jax.experimental import pallas as pl
from jax.experimental.pallas import tpu as pltpu
from jax.sharding import PartitionSpec as P

MESH = pl.DeviceIdType.MESH
SUB = 8
MODES = 16
TAPS = 3
RIM = TAPS - 1
RUNS = 4
WIDE = 4
HALF = RUNS * WIDE
F32 = jnp.float32
BF16 = jnp.bfloat16


def rounded(value):
    return value.astype(BF16).astype(F32)


def one_minus_exp(x):
    series = jnp.ones_like(x)
    for k in range(10, 1, -1):
        series = 1.0 - x * (1.0 / k) * series
    return jnp.where(x < 0.5, x * series, 1.0 - jnp.exp(-x))


def kernel(
    n,
    local_len,
    own,
    proj_ref,
    cot_ref,
    sw_hbm,
    decay_hbm,
    res_hbm,
    skip_hbm,
    land,
    all_short,
    gres_hbm,
    gdec_hbm,
    gskip_hbm,
    rx,
    so,
    xt,
    qs,
    ks,
    vs,
    us,
    gs,
    cv,
    gf,
    kept,
    sw,
    filt,
    par,
    wt,
    lam,
    coef,
    tots,
    ins,
    ends,
    edge,
    edge_in,
    sums,
    sums_in,
    shorts,
    gres,
    gskip,
    pacc,
    racc,
    send_sem,
    recv_sem,
    local_sem,
):
    me = lax.axis_index("context")
    length = n * local_len
    steps = local_len // SUB
    chans = 2 * own
    root = math.sqrt(length)
    run_len = WIDE * local_len
    side = lax.rem(me // WIDE, 2)
    my_x = me // (2 * WIDE)
    my_w = lax.rem(me, WIDE)
    my_slot = my_x * WIDE + my_w
    partner = me + WIDE * (1 - 2 * side)
    is_a = side == 0

    def each_peer(body):
        def step(t, carry):
            slot = lax.rem(my_slot + t, HALF)
            x, w = slot // WIDE, lax.rem(slot, WIDE)
            body(slot, x, w, (2 * x + side) * WIDE + w)
            return carry

        lax.fori_loop(1, HALF, step, 0)

    def remote(src, dst, k, device):
        return pltpu.make_async_remote_copy(
            src_ref=src,
            dst_ref=dst,
            send_sem=send_sem.at[k],
            recv_sem=recv_sem.at[k],
            device_id={"context": device},
            device_id_type=MESH,
        )

    def arrived(ref, k):
        pltpu.make_async_copy(ref, ref, recv_sem.at[k]).wait()

    def left(ref, k):
        pltpu.make_async_copy(ref, ref, send_sem.at[k]).wait()

    barrier = pltpu.get_barrier_semaphore()
    pl.semaphore_signal(barrier, inc=1, device_id={"context": partner}, device_id_type=MESH)
    each_peer(
        lambda slot, x, w, device: pl.semaphore_signal(
            barrier, inc=1, device_id={"context": device}, device_id_type=MESH
        )
    )
    small = [
        pltpu.make_async_copy(sw_hbm, sw, local_sem.at[0]),
        pltpu.make_async_copy(decay_hbm, filt.at[0], local_sem.at[1]),
        pltpu.make_async_copy(res_hbm, filt.at[1], local_sem.at[2]),
        pltpu.make_async_copy(skip_hbm, filt.at[2, pl.ds(0, 1)], local_sem.at[3]),
    ]
    keep = [
        pltpu.make_async_copy(
            proj_ref.at[:, my_x, :, my_w], rx.at[my_slot, pl.ds(0, 3)], local_sem.at[4]
        ),
        pltpu.make_async_copy(cot_ref.at[my_x, :, my_w], rx.at[my_slot, 3], local_sem.at[5]),
    ]
    for copy in small + keep:
        copy.start()

    lane = lax.broadcasted_iota(jnp.int32, (1, 128), 1)
    group = lane // chans
    sub_row = lax.broadcasted_iota(jnp.int32, (SUB, 128), 0)
    corner = jnp.logical_and(sub_row == 0, group == 0)

    def group_sum(rows):
        width = chans
        while width < 128:
            rows = rows + pltpu.roll(rows, width, 1)
            width *= 2
        return rows

    def to_group(rows, here, there):
        shift = ((there - here) * chans) % 128
        return pltpu.roll(rows, shift, 1) if shift else rows

    def packed(tiles, here):
        total = None
        for jt in range(RUNS):
            piece = jnp.where(group == jt, to_group(tiles[jt], here, jt), 0.0)
            total = piece if total is None else total + piece
        return total

    def repeated(rows, jt):
        return group_sum(jnp.where(group == jt, rows, 0.0))

    def before(rows):
        return jnp.where(group >= 1, pltpu.roll(rows, chans, 1), 0.0)

    def after(rows):
        return jnp.where(group < RUNS - 1, pltpu.roll(rows, 128 - chans, 1), 0.0)

    for copy in small:
        copy.wait()
    pl.semaphore_wait(barrier, HALF)

    remote(filt.at[pl.ds(0, 3)], filt.at[pl.ds(3, 3)], 3, partner).start()

    def send_kv(slot, x, w, device):
        remote(proj_ref.at[pl.ds(1, 2), x, :, w], rx.at[my_slot, pl.ds(1, 2)], 0, device).start()

    def send_q_cot(slot, x, w, device):
        remote(proj_ref.at[0, x, :, w], rx.at[my_slot, 0], 1, device).start()
        remote(cot_ref.at[x, :, w], rx.at[my_slot, 3], 2, device).start()

    each_peer(send_kv)
    each_peer(send_q_cot)

    for i in range(3):
        rows = jnp.concatenate(
            [
                sw[i, :, pl.ds(pl.multiple_of(my_x * 128, 128), 128)],
                jnp.zeros((SUB - TAPS, 128), F32),
            ],
            axis=0,
        )
        rows = pltpu.roll(rows, lax.rem(128 - my_w * own, 128), 1)
        rows = jnp.where(lane < own, rows, 0.0) + pltpu.roll(
            jnp.where(jnp.logical_and(lane >= 64, lane < 64 + own), rows, 0.0), 64 + own, 1
        )
        rows = group_sum(rows)
        for j in range(TAPS):
            wt[TAPS * i + j] = jnp.broadcast_to(rows[j : j + 1, :], (SUB, 128))
    for copy in keep:
        copy.wait()
    arrived(filt.at[pl.ds(3, 3)], 3)
    par[...] = jnp.zeros_like(par)
    for k in range(2):
        mine, theirs = filt[k], filt[3 + k]
        first, second = jnp.where(is_a, mine, theirs), jnp.where(is_a, theirs, mine)
        for g in range(128 // chans):
            par[k, g * chans : g * chans + own, 0:MODES] = first
            par[k, g * chans + own : (g + 1) * chans, 0:MODES] = second
    mine, theirs = filt[2, 0:1, :], filt[5, 0:1, :]
    par[2, 0:1, 0:own] = jnp.where(is_a, mine, theirs)
    par[2, 1:2, 0:own] = jnp.where(is_a, theirs, mine)
    skip_row = group_sum(par[2, 0:1, :] + pltpu.roll(par[2, 1:2, :], own, 1))
    wt[9] = jnp.broadcast_to(skip_row, (SUB, 128))
    per = par[0].T[0:MODES, :] * (1.0 / length)
    residue = par[1].T[0:MODES, :]
    scale = jnp.sqrt(one_minus_exp(2.0 * per))
    coef_rows = residue * scale
    lam_rows = jnp.exp(-per)
    inv_lam = jnp.exp(per)
    par[3, 0:MODES, :] = per
    for m in range(MODES):
        lam[m] = jnp.broadcast_to(lam_rows[m : m + 1, :], (SUB, 128))
        coef[m] = jnp.broadcast_to(coef_rows[m : m + 1, :], (SUB, 128))

    def power(span):
        return jnp.exp(per * (-1.0 * span))

    sub_spans = [1, 2, 4]
    run_span, pair_span = power(run_len), power(2 * run_len)
    up_span = jnp.exp(per * (-1.0 * local_len) * group.astype(F32))
    down_span = jnp.exp(per * (-1.0 * local_len) * (WIDE - 1 - group).astype(F32))

    row = lax.broadcasted_iota(jnp.int32, (local_len, local_len), 0)
    column = lax.broadcasted_iota(jnp.int32, (local_len, local_len), 1)
    order = jnp.where(column == lax.rem(row, SUB) * steps + row // SUB, 1.0, 0.0).astype(BF16)

    def turn(arrays):
        def tile(jt):
            for a in arrays:
                block = rx[pl.ds(WIDE * jt, WIDE), a].reshape(128, local_len)
                rows = lax.dot_general(
                    order, block, (((1,), (1,)), ((), ())), preferred_element_type=F32
                ).reshape(steps, SUB, 128)
                xt[a, jt, RIM : RIM + steps] = rows
                if a < 3:
                    for i in range(RIM):
                        moved = pltpu.roll(rows[steps - RIM + i], 1, 0)
                        first = jnp.where(group == 0, 0.0, pltpu.roll(moved, chans, 1))
                        xt[a, jt, i] = jnp.where(sub_row == 0, first, moved)

        for jt in range(RUNS):
            tile(jt)

    def turn_back(rows):
        flat = rows.astype(BF16).reshape(local_len, 128)
        return (
            lax.dot_general(flat, order, (((0,), (0,)), ((), ())), preferred_element_type=F32)
            .astype(BF16)
            .reshape(WIDE, 2, own, local_len)
        )

    def path(a, jt, p):
        total = None
        for j in range(TAPS):
            term = wt[TAPS * a + j] * xt[a, jt, RIM + p - j]
            total = term if total is None else total + term
        return total

    def last_rows(a):
        return packed(
            [
                jnp.concatenate(
                    [xt[a, jt, steps + i, SUB - 1 : SUB, :] for i in range(RIM)], axis=0
                )
                for jt in range(RUNS)
            ],
            WIDE - 1,
        )

    def first_rows(a):
        return packed(
            [
                jnp.concatenate([xt[a, jt, RIM + i, 0:1, :] for i in range(RIM)], axis=0)
                for jt in range(RUNS)
            ],
            0,
        )

    def edge_path(a, first, last):
        w = [wt[TAPS * a + j][0:1, :] for j in range(TAPS)]
        return (
            w[0] * first[0:1] + w[1] * last[1:2] + w[2] * last[0:1],
            w[0] * first[1:2] + w[1] * first[0:1] + w[2] * last[1:2],
        )

    def mine_before(rows):
        return jnp.where(is_a, rows, before(rows))

    def theirs_before(rows):
        return jnp.where(is_a, before(rows), rows)

    def theirs_after(rows):
        return jnp.where(is_a, rows, after(rows))

    def fill_rim(a, rows):
        for jt in range(RUNS):
            rim = to_group(rows, jt, 0)
            for i in range(RIM):
                xt[a, jt, i] = jnp.where(
                    corner, jnp.broadcast_to(rim[i : i + 1, :], (SUB, 128)), xt[a, jt, i]
                )

    many = 8

    def block_ends(k, signal, reverse):
        def some(at, carry):
            jt = at // (MODES // many)
            first = lax.rem(at, MODES // many) * many
            lams = [lam[first + i] for i in range(many)]
            state = [None] * many
            for p in reversed(range(steps)) if reverse else range(steps):
                x = signal[jt, p]
                for i in range(many):
                    state[i] = x if state[i] is None else lams[i] * state[i] + x
            for i in range(many):
                pers = jnp.broadcast_to(par[3, pl.ds(first + i, 1), :], (SUB, 128))
                s = state[i]
                for d in sub_spans:
                    factor = jnp.exp(pers * (-1.0 * steps * d))
                    if reverse:
                        moved = jnp.where(sub_row < SUB - d, pltpu.roll(s, SUB - d, 0), 0.0)
                    else:
                        moved = jnp.where(sub_row >= d, pltpu.roll(s, d, 0), 0.0)
                    s = s + factor * moved
                if reverse:
                    ins[k, jt, first + i] = jnp.where(
                        sub_row < SUB - 1, pltpu.roll(s, SUB - 1, 0), 0.0
                    )
                    tots[k, jt, pl.ds(first + i, 1), :] = s[0:1, :]
                else:
                    ins[k, jt, first + i] = jnp.where(sub_row >= 1, pltpu.roll(s, 1, 0), 0.0)
                    tots[k, jt, pl.ds(first + i, 1), :] = s[SUB - 1 : SUB, :]
            return carry

        lax.fori_loop(0, RUNS * (MODES // many), some, 0)

    def run_ends(k, reverse):
        tiles = []
        for jt in range(RUNS):
            s = tots[k, jt]
            for d in (1, 2):
                if reverse:
                    moved = jnp.where(group < WIDE - d, pltpu.roll(s, 128 - chans * d, 1), 0.0)
                else:
                    moved = jnp.where(group >= d, pltpu.roll(s, chans * d, 1), 0.0)
                s = s + power(local_len * d) * moved
            tiles.append(s)
            tots[k, jt] = after(s) if reverse else before(s)
        return packed(tiles, 0 if reverse else WIDE - 1)

    arrived(rx.at[pl.ds(0, HALF - 1), pl.ds(1, 2)], 0)
    turn((1, 2))

    def gate_kv(jt, carry):
        for p in range(steps):
            key, value = path(1, jt, p), path(2, jt, p)
            u = rounded(key * value)
            ks[jt, p] = key
            vs[jt, p] = value
            us[jt, p] = jnp.where(corner, 0.0, u) if p < 2 else u
        return carry

    lax.fori_loop(0, RUNS, gate_kv, 0)
    block_ends(0, us, False)
    my_f = run_ends(0, False)
    k_last, v_last = last_rows(1), last_rows(2)
    k_first, v_first = first_rows(1), first_rows(2)
    edge[0, 0:MODES, :] = my_f
    edge[0, MODES : MODES + 8, :] = jnp.concatenate([k_last, v_last, k_first, v_first], axis=0)
    remote(edge.at[0], edge_in.at[0], 4, partner).start()

    arrived(rx.at[pl.ds(0, HALF - 1), 0], 1)
    arrived(rx.at[pl.ds(0, HALF - 1), 3], 2)
    turn((0, 3))

    def gate_q(jt, carry):
        for p in range(steps):
            query = path(0, jt, p)
            g = rounded(xt[3, jt, RIM + p] * query)
            qs[jt, p] = query
            gs[jt, p] = jnp.where(corner, 0.0, g) if p < 2 else g
        return carry

    q_last, q_first, c_first = last_rows(0), first_rows(0), first_rows(3)
    edge[1, MODES : MODES + 8, :] = jnp.concatenate(
        [q_last, q_first, c_first, jnp.zeros((2, 128), F32)], axis=0
    )
    remote(
        edge.at[1, pl.ds(MODES, 8)], edge_in.at[1, pl.ds(MODES, 8)], 10, partner
    ).start()
    lax.fori_loop(0, RUNS, gate_q, 0)
    block_ends(1, gs, True)
    my_b = run_ends(1, True)
    edge[1, 0:MODES, :] = my_b
    remote(edge.at[1, pl.ds(0, MODES)], edge_in.at[1, pl.ds(0, MODES)], 5, partner).start()

    arrived(edge_in.at[0], 4)
    their_f = edge_in[0, 0:MODES, :]
    rows = edge_in[0, MODES : MODES + 8, :]
    tk_last, tv_last, tk_first, tv_first = rows[0:2], rows[2:4], rows[4:6], rows[6:8]
    fill_rim(1, theirs_before(tk_last))
    fill_rim(2, theirs_before(tv_last))

    def regate_kv(jt, carry):
        for p in range(2):
            key, value = path(1, jt, p), path(2, jt, p)
            ks[jt, p] = key
            vs[jt, p] = value
            us[jt, p] = rounded(key * value)
        return carry

    lax.fori_loop(0, RUNS, regate_kv, 0)
    my_k = edge_path(1, k_first, theirs_before(tk_last))
    my_v = edge_path(2, v_first, theirs_before(tv_last))
    their_k = edge_path(1, tk_first, mine_before(k_last))
    their_v = edge_path(2, tv_first, mine_before(v_last))
    my_u = [rounded(k * v) for k, v in zip(my_k, my_v)]
    their_u = [rounded(k * v) for k, v in zip(their_k, their_v)]
    late = (power(run_len - 1), power(run_len - 2))
    my_f = my_f + late[0] * my_u[0] + late[1] * my_u[1]
    their_f = their_f + late[0] * their_u[0] + late[1] * their_u[1]
    a_f, b_f = jnp.where(is_a, my_f, their_f), jnp.where(is_a, their_f, my_f)
    scan = run_span * a_f + b_f
    scan = scan + pair_span * before(scan)
    scan = scan + power(4 * run_len) * jnp.where(group >= 2, pltpu.roll(scan, 2 * chans, 1), 0.0)
    into_a = before(scan)
    carry_f = jnp.where(is_a, into_a, run_span * into_a + a_f)
    next_f = run_span * carry_f + my_f
    whole_f = carry_f + inv_lam * (my_u[0] + inv_lam * my_u[1])
    for jt in range(RUNS):
        tots[0, jt] = tots[0, jt] + up_span * repeated(whole_f, jt)
        ends[jt] = repeated(carry_f, jt)

    def in_state(k, jt, m):
        pers = jnp.broadcast_to(par[3, pl.ds(m, 1), :], (SUB, 128))
        into = jnp.broadcast_to(tots[k, jt, pl.ds(m, 1), :], (SUB, 128))
        away = (sub_row if k == 0 else SUB - 1 - sub_row).astype(F32)
        state = ins[k, jt, m] + jnp.exp(pers * (-1.0 * steps) * away) * into
        if k == 0:
            exact = jnp.broadcast_to(ends[jt, pl.ds(m, 1), :], (SUB, 128))
            state = jnp.where(corner, exact, state)
        return state

    def summed(parts):
        while len(parts) > 1:
            parts = [parts[i] + parts[i + 1] for i in range(0, len(parts), 2)]
        return parts[0]

    def conv_tile(jt, carry):
        def some(at, totals):
            totals = list(totals)
            first = at * many
            lams = [lam[first + i] for i in range(many)]
            coefs = [coef[first + i] for i in range(many)]
            state = [in_state(0, jt, first + i) for i in range(many)]
            for p in range(steps):
                u = us[jt, p]
                for i in range(many):
                    state[i] = lams[i] * state[i] + u
                    kept[jt, first + i, p] = state[i]
                totals[p] = totals[p] + summed([coefs[i] * state[i] for i in range(many)])
            return tuple(totals)

        start = tuple(wt[9] * us[jt, p] for p in range(steps))
        totals = lax.fori_loop(0, MODES // many, some, start)
        for p in range(steps):
            cv[jt, p] = rounded(totals[p])
        return carry

    lax.fori_loop(0, RUNS, conv_tile, 0)

    arrived(edge_in.at[1, pl.ds(MODES, 8)], 10)
    rows = edge_in[1, MODES : MODES + 8, :]
    tq_last, tq_first, tc_first = rows[0:2], rows[2:4], rows[4:6]
    fill_rim(0, theirs_before(tq_last))

    def regate_q(jt, carry):
        for p in range(2):
            query = path(0, jt, p)
            qs[jt, p] = query
            gs[jt, p] = rounded(xt[3, jt, RIM + p] * query)
        for p in range(steps):
            gf[0, jt, p] = xt[3, jt, RIM + p] * cv[jt, p]
        return carry

    lax.fori_loop(0, RUNS, regate_q, 0)
    next_u = [theirs_after(u) for u in their_u]
    next_c = theirs_after(tc_first)
    state0 = lam_rows * next_f + next_u[0]
    state1 = lam_rows * state0 + next_u[1]
    beyond = [[], [], []]
    for i, state in enumerate((state0, state1)):
        conv = rounded(
            jnp.sum(coef_rows * state, axis=0, keepdims=True) + skip_row * next_u[i]
        )
        beyond[0].append(next_c[i : i + 1] * conv)

    def gf_rim(a):
        for jt in range(RUNS):
            for i in range(RIM):
                rim = jnp.broadcast_to(to_group(beyond[a][i], jt, WIDE - 1), (SUB, 128))
                moved = pltpu.roll(gf[a, jt, i], SUB - 1, 0)
                last = jnp.where(group == WIDE - 1, rim, pltpu.roll(moved, 128 - chans, 1))
                gf[a, jt, steps + i] = jnp.where(sub_row == SUB - 1, last, moved)

    def grad_path(a, jt):
        w = [wt[TAPS * a + j] for j in range(TAPS)]
        rows = []
        for p in range(steps):
            total = w[0] * gf[a, jt, p]
            for j in range(1, TAPS):
                total = total + w[j] * gf[a, jt, p + j]
            rows.append(total)
        so[pl.ds(WIDE * jt, WIDE), 1 + a] = turn_back(jnp.stack(rows))

    def send_tile(jt, arrays, k):
        for w in range(WIDE):
            slot = WIDE * jt + w

            @pl.when(slot != my_slot)
            def _():
                remote(
                    so.at[slot, arrays],
                    land.at[my_slot, arrays],
                    k,
                    (2 * jt + side) * WIDE + w,
                ).start()

    gf_rim(0)

    def first_results(t, carry):
        jt = lax.rem(my_x + 1 + t, RUNS)
        so[pl.ds(WIDE * jt, WIDE), 0] = turn_back(
            jnp.stack([qs[jt, p] * cv[jt, p] for p in range(steps)])
        )
        grad_path(0, jt)
        send_tile(jt, pl.ds(0, 2), 7)
        return carry

    lax.fori_loop(0, RUNS, first_results, 0)

    my_q = edge_path(0, q_first, theirs_before(tq_last))
    their_q = edge_path(0, tq_first, mine_before(q_last))
    my_g = [rounded(my_q[i] * c_first[i : i + 1]) for i in range(2)]
    their_g = [rounded(their_q[i] * tc_first[i : i + 1]) for i in range(2)]
    arrived(edge_in.at[1, pl.ds(0, MODES)], 5)
    their_b = edge_in[1, 0:MODES, :]
    my_b = my_b + my_g[0] + lam_rows * my_g[1]
    their_b = their_b + their_g[0] + lam_rows * their_g[1]
    a_b, b_b = jnp.where(is_a, my_b, their_b), jnp.where(is_a, their_b, my_b)
    scan = a_b + run_span * b_b
    scan = scan + pair_span * after(scan)
    scan = scan + power(4 * run_len) * jnp.where(
        group < RUNS - 2, pltpu.roll(scan, 128 - 2 * chans, 1), 0.0
    )
    into_b = after(scan)
    carry_b = jnp.where(is_a, run_span * into_b + b_b, into_b)
    for jt in range(RUNS):
        tots[1, jt] = tots[1, jt] + down_span * repeated(carry_b, jt)

    next_g = [theirs_after(g) for g in their_g]
    for i, back in enumerate((carry_b, inv_lam * (carry_b - next_g[0]))):
        back = rounded(jnp.sum(coef_rows * back, axis=0, keepdims=True) + skip_row * next_g[i])
        beyond[1].append(back * theirs_after(their_v[i]))
        beyond[2].append(back * theirs_after(their_k[i]))

    def back_tile(jt, carry):
        def some(at, totals):
            totals = list(totals)
            first = at * many
            lams = [lam[first + i] for i in range(many)]
            coefs = [coef[first + i] for i in range(many)]
            state = [in_state(1, jt, first + i) for i in range(many)]
            for i in range(many):
                ins[1, jt, first + i] = state[i]
            for p in reversed(range(steps)):
                g = gs[jt, p]
                for i in range(many):
                    state[i] = lams[i] * state[i] + g
                totals[p] = totals[p] + summed([coefs[i] * state[i] for i in range(many)])
            return tuple(totals)

        carry = list(carry)
        start = tuple(wt[9] * gs[jt, p] for p in range(steps))
        totals = lax.fori_loop(0, MODES // many, some, start)
        for p in range(steps):
            back = rounded(totals[p])
            grads = (gf[0, jt, p], back * vs[jt, p], back * ks[jt, p])
            gf[1, jt, p] = grads[1]
            gf[2, jt, p] = grads[2]
            for a in range(3):
                for j in range(TAPS):
                    carry[TAPS * a + j] += grads[a] * xt[a, jt, RIM + p - j]
            carry[9] += us[jt, p] * gs[jt, p]
        return tuple(carry)

    found = lax.fori_loop(
        0, RUNS, back_tile, tuple(jnp.zeros((SUB, 128), F32) for _ in range(10))
    )

    taps = [group_sum(jnp.sum(part, axis=0, keepdims=True)) * (1.0 / root) for part in found]
    sides = []
    for r in range(3):
        side_row = jnp.zeros((1, 128), F32)
        for g in range(4):
            if 4 * r + g < 3 * TAPS:
                side_row = jnp.where(group == g, taps[4 * r + g], side_row)
        sides.append(side_row)
    shorts[...] = jnp.concatenate(sides + [jnp.zeros((1, 128), F32)], axis=0)

    def send_short(t, carry):
        remote(shorts, all_short.at[me], 9, lax.rem(me + t, n)).start()
        return carry

    gf_rim(1)
    gf_rim(2)

    def last_results(t, carry):
        @pl.when(t < 2)
        def _():
            lax.fori_loop(jnp.maximum(16 * t, 1), 16 * t + 16, send_short, 0)

        jt = lax.rem(my_x + 1 + t, RUNS)
        grad_path(1, jt)
        grad_path(2, jt)
        send_tile(jt, pl.ds(2, 2), 8)
        return carry

    lax.fori_loop(0, RUNS, last_results, 0)
    keep_out = [pltpu.make_async_copy(so.at[my_slot], land.at[my_slot], local_sem.at[0])]
    keep_out[0].start()

    pacc[...] = jnp.zeros_like(pacc)
    racc[...] = jnp.zeros_like(racc)
    few = 4

    def mode_sums(at, carry):
        jt = at // (MODES // few)
        first = lax.rem(at, MODES // few) * few
        lams = [lam[first + i] for i in range(few)]
        state = [ins[1, jt, first + i] for i in range(few)]
        plain = [None] * few
        ramped = [None] * few
        for p in reversed(range(steps)):
            g = gs[jt, p]
            for i in range(few):
                fwd = kept[jt, first + i, p]
                flat = g * fwd
                ramp = state[i] * fwd
                plain[i] = flat if plain[i] is None else plain[i] + flat
                ramped[i] = ramp if ramped[i] is None else ramped[i] + ramp
                state[i] = lams[i] * state[i] + g
        for i in range(few):
            pacc[first + i] += plain[i]
            racc[first + i] += ramped[i]
        return carry

    lax.fori_loop(0, RUNS * (MODES // few), mode_sums, 0)
    my_plain = group_sum(
        jnp.concatenate([jnp.sum(pacc[m], axis=0, keepdims=True) for m in range(MODES)], axis=0)
    )
    my_ramped = group_sum(
        jnp.concatenate([jnp.sum(racc[m], axis=0, keepdims=True) for m in range(MODES)], axis=0)
    )
    sums[0:MODES, :] = my_plain
    sums[MODES : 2 * MODES, :] = my_ramped
    sums[2 * MODES : 2 * MODES + 8, :] = jnp.broadcast_to(taps[9], (SUB, 128))
    remote(sums, sums_in, 6, partner).start()

    arrived(sums_in, 6)
    plain = my_plain + sums_in[0:MODES, :]
    ramped = lam_rows * (my_ramped + sums_in[MODES : 2 * MODES, :])
    skips = taps[9] + sums_in[2 * MODES : 2 * MODES + 1, :]
    gskip[...] = jnp.where(is_a, skips[:, 0:own], skips[:, own : 2 * own])
    grad_res = scale * plain / root
    grad_dec = residue * (jnp.exp(-2.0 * per) / scale * plain - scale * ramped) / (length * root)
    par[0, 0:MODES, :] = grad_res
    par[1, 0:MODES, :] = grad_dec
    for k in range(2):
        turned = par[k].T
        gres[k] = jnp.where(is_a, turned[0:own, 0:MODES], turned[own : 2 * own, 0:MODES])
    for at, (src, dst) in enumerate(
        (
            (shorts, all_short.at[me]),
            (gres.at[0], gres_hbm),
            (gres.at[1], gdec_hbm),
            (gskip, gskip_hbm),
        )
    ):
        keep_out.append(pltpu.make_async_copy(src, dst, local_sem.at[1 + at]))
        keep_out[-1].start()

    arrived(all_short.at[pl.ds(0, n - 1)], 9)
    for copy in keep_out:
        copy.wait()
    most = pl.ds(0, HALF - 1)
    arrived(so.at[most, pl.ds(0, 2)], 7)
    arrived(so.at[most, pl.ds(2, 2)], 8)
    left(rx.at[most, pl.ds(1, 2)], 0)
    left(rx.at[most, 0], 1)
    left(rx.at[most, 3], 2)
    left(filt.at[pl.ds(0, 3)], 3)
    left(edge.at[0], 4)
    left(edge.at[1, pl.ds(0, MODES)], 5)
    left(edge.at[1, pl.ds(MODES, 8)], 10)
    left(sums, 6)
    left(so.at[most, pl.ds(0, 2)], 7)
    left(so.at[most, pl.ds(2, 2)], 8)
    left(all_short.at[pl.ds(0, n - 1)], 9)


def write_out(land, parts, res, dec, skip, out, gproj, gshort, gres, gdec, gskip):
    own = land.shape[3]
    place = lax.broadcasted_iota(jnp.int32, (1, 128), 1) // own
    for x in range(RUNS):
        for half in range(2):
            for w in range(WIDE):
                out[x, half, w] = land[WIDE * x + w, 0, half]
                for a in range(3):
                    gproj[a, x, half, w] = land[WIDE * x + w, 1 + a, half]
        rows = [jnp.zeros((4, 128), F32) for _ in range(4)]
        for w in range(WIDE):
            at = 2 * WIDE * x + w
            both = parts[at] + parts[at + WIDE]
            for g in range(4):
                low = (own * w - 2 * own * g) % 128
                high = (64 + own * w - own - 2 * own * g) % 128
                low = pltpu.roll(both, low, 1) if low else both
                high = pltpu.roll(both, high, 1) if high else both
                rows[g] = jnp.where(place == w, low, jnp.where(place == w + WIDE, high, rows[g]))
        for k in range(3 * TAPS):
            gshort[k // TAPS, k % TAPS : k % TAPS + 1, 128 * x : 128 * (x + 1)] = rows[k % 4][
                k // 4 : k // 4 + 1, :
            ]
    gres[...] = res[...]
    gdec[...] = dec[...]
    gskip[...] = skip[...]


def per_device(projected, short_weight, residues, decay_rates, skip_weight, cotangent):
    n = lax.axis_size("context")
    channels, local_len = cotangent.shape
    own = channels // n
    steps = local_len // SUB
    vmem = pl.BlockSpec(memory_space=pltpu.VMEM)
    hbm = pl.BlockSpec(memory_space=pltpu.HBM)
    stepped = pltpu.VMEM((RUNS, steps, SUB, 128), F32)
    blocks = (RUNS, 2, WIDE, own, local_len)
    small = (
        jax.ShapeDtypeStruct((own, MODES), F32),
        jax.ShapeDtypeStruct((own, MODES), F32),
        jax.ShapeDtypeStruct((1, own), F32),
    )
    results = pl.pallas_call(
        functools.partial(kernel, n, local_len, own),
        out_shape=(
            jax.ShapeDtypeStruct((HALF, 4, 2, own, local_len), BF16),
            jax.ShapeDtypeStruct((n, 4, 128), F32),
        )
        + small,
        in_specs=[hbm] * 6,
        out_specs=(hbm,) * 5,
        scratch_shapes=[
            pltpu.VMEM((HALF, 4, 2, own, local_len), BF16),
            pltpu.VMEM((HALF, 4, 2, own, local_len), BF16),
            pltpu.VMEM((4, RUNS, RIM + steps, SUB, 128), F32),
            stepped,
            stepped,
            stepped,
            stepped,
            stepped,
            stepped,
            pltpu.VMEM((3, RUNS, steps + RIM, SUB, 128), F32),
            pltpu.VMEM((RUNS, MODES, steps, SUB, 128), F32),
            pltpu.VMEM((3, TAPS, channels), F32),
            pltpu.VMEM((6, own, MODES), F32),
            pltpu.VMEM((4, 128, 128), F32),
            pltpu.VMEM((10, SUB, 128), F32),
            pltpu.VMEM((MODES, SUB, 128), F32),
            pltpu.VMEM((MODES, SUB, 128), F32),
            pltpu.VMEM((2, RUNS, MODES, 128), F32),
            pltpu.VMEM((2, RUNS, MODES, SUB, 128), F32),
            pltpu.VMEM((RUNS, MODES, 128), F32),
            pltpu.VMEM((2, MODES + 8, 128), F32),
            pltpu.VMEM((2, MODES + 8, 128), F32),
            pltpu.VMEM((8 + 2 * MODES, 128), F32),
            pltpu.VMEM((8 + 2 * MODES, 128), F32),
            pltpu.VMEM((4, 128), F32),
            pltpu.VMEM((2, own, MODES), F32),
            pltpu.VMEM((1, own), F32),
            pltpu.VMEM((MODES, SUB, 128), F32),
            pltpu.VMEM((MODES, SUB, 128), F32),
            pltpu.SemaphoreType.DMA((11,)),
            pltpu.SemaphoreType.DMA((11,)),
            pltpu.SemaphoreType.DMA((6,)),
        ],
        compiler_params=pltpu.CompilerParams(
            collective_id=0, has_side_effects=True, vmem_limit_bytes=56 * 1024 * 1024
        ),
    )(
        projected.reshape((3,) + blocks),
        cotangent.reshape(blocks),
        short_weight.transpose(0, 2, 1),
        decay_rates,
        residues,
        skip_weight.reshape(1, -1),
    )
    output, grad_projected, grad_short, grad_res, grad_dec, grad_skip = pl.pallas_call(
        write_out,
        out_shape=(
            jax.ShapeDtypeStruct(blocks, BF16),
            jax.ShapeDtypeStruct((3,) + blocks, BF16),
            jax.ShapeDtypeStruct((3, TAPS, channels), F32),
        )
        + small,
        in_specs=[vmem] * 5,
        out_specs=(vmem,) * 6,
    )(*results)
    return (
        output.reshape(channels, local_len),
        grad_projected.reshape(3, channels, local_len),
        grad_short.transpose(0, 2, 1),
        grad_res,
        grad_dec,
        grad_skip.reshape(-1),
    )


def solution(mesh):
    return jax.shard_map(
        per_device,
        mesh=mesh,
        in_specs=(
            P(None, "tensor", "context"),
            P(None, "tensor", None),
            P(("tensor", "context"), None),
            P(("tensor", "context"), None),
            P(("tensor", "context")),
            P("tensor", "context"),
        ),
        out_specs=(
            P("tensor", "context"),
            P(None, "tensor", "context"),
            P(None, "tensor", None),
            P(("tensor", "context"), None),
            P(("tensor", "context"), None),
            P(("tensor", "context")),
        ),
        check_vma=False,
    )
```

```python
import functools
import math

import jax
import jax.numpy as jnp
from jax import lax
from jax.experimental import pallas as pl
from jax.experimental.pallas import tpu as pltpu
from jax.sharding import PartitionSpec as P

MESH = pl.DeviceIdType.MESH
SUB = 8
MODES = 16
TAPS = 3
RIM = TAPS - 1
RUNS = 4
WIDE = 4
HALF = RUNS * WIDE
F32 = jnp.float32
BF16 = jnp.bfloat16


def rounded(value):
    return value.astype(BF16).astype(F32)


def one_minus_exp(x):
    series = jnp.ones_like(x)
    for k in range(10, 1, -1):
        series = 1.0 - x * (1.0 / k) * series
    return jnp.where(x < 0.5, x * series, 1.0 - jnp.exp(-x))


def kernel(
    n,
    local_len,
    own,
    proj_hbm,
    cot_hbm,
    sw_hbm,
    decay_hbm,
    res_hbm,
    skip_hbm,
    land,
    all_short,
    gres_hbm,
    gdec_hbm,
    gskip_hbm,
    proj_ref,
    cot_ref,
    rx,
    so,
    xt,
    qs,
    ks,
    vs,
    us,
    gs,
    cv,
    gf,
    kept,
    sw,
    filt,
    par,
    wt,
    lam,
    coef,
    tots,
    ins,
    ends,
    edge,
    edge_in,
    sums,
    sums_in,
    shorts,
    gres,
    gskip,
    pacc,
    racc,
    send_sem,
    recv_sem,
    local_sem,
):
    me = lax.axis_index("context")
    length = n * local_len
    steps = local_len // SUB
    chans = 2 * own
    root = math.sqrt(length)
    run_len = WIDE * local_len
    side = lax.rem(me // WIDE, 2)
    my_x = me // (2 * WIDE)
    my_w = lax.rem(me, WIDE)
    my_slot = my_x * WIDE + my_w
    partner = me + WIDE * (1 - 2 * side)
    is_a = side == 0

    def each_peer(body):
        def step(t, carry):
            slot = lax.rem(my_slot + t, HALF)
            x, w = slot // WIDE, lax.rem(slot, WIDE)
            body(slot, x, w, (2 * x + side) * WIDE + w)
            return carry

        lax.fori_loop(1, HALF, step, 0)

    def remote(src, dst, k, device):
        return pltpu.make_async_remote_copy(
            src_ref=src,
            dst_ref=dst,
            send_sem=send_sem.at[k],
            recv_sem=recv_sem.at[k],
            device_id={"context": device},
            device_id_type=MESH,
        )

    def arrived(ref, k):
        pltpu.make_async_copy(ref, ref, recv_sem.at[k]).wait()

    def left(ref, k):
        pltpu.make_async_copy(ref, ref, send_sem.at[k]).wait()

    barrier = pltpu.get_barrier_semaphore()
    pl.semaphore_signal(barrier, inc=1, device_id={"context": partner}, device_id_type=MESH)
    each_peer(
        lambda slot, x, w, device: pl.semaphore_signal(
            barrier, inc=1, device_id={"context": device}, device_id_type=MESH
        )
    )
    small = [
        pltpu.make_async_copy(sw_hbm, sw, local_sem.at[0]),
        pltpu.make_async_copy(decay_hbm, filt.at[0], local_sem.at[1]),
        pltpu.make_async_copy(res_hbm, filt.at[1], local_sem.at[2]),
        pltpu.make_async_copy(skip_hbm, filt.at[2, pl.ds(0, 1)], local_sem.at[3]),
    ]
    keep = [
        pltpu.make_async_copy(
            proj_ref.at[:, my_x, :, my_w], rx.at[my_slot, pl.ds(0, 3)], local_sem.at[4]
        ),
        pltpu.make_async_copy(cot_ref.at[my_x, :, my_w], rx.at[my_slot, 3], local_sem.at[5]),
    ]
    whole = [
        pltpu.make_async_copy(proj_hbm, proj_ref, local_sem.at[6]),
        pltpu.make_async_copy(cot_hbm, cot_ref, local_sem.at[7]),
    ]
    for copy in whole + small:
        copy.start()

    lane = lax.broadcasted_iota(jnp.int32, (1, 128), 1)
    group = lane // chans
    sub_row = lax.broadcasted_iota(jnp.int32, (SUB, 128), 0)
    corner = jnp.logical_and(sub_row == 0, group == 0)

    def group_sum(rows):
        width = chans
        while width < 128:
            rows = rows + pltpu.roll(rows, width, 1)
            width *= 2
        return rows

    def to_group(rows, here, there):
        shift = ((there - here) * chans) % 128
        return pltpu.roll(rows, shift, 1) if shift else rows

    def packed(tiles, here):
        total = None
        for jt in range(RUNS):
            piece = jnp.where(group == jt, to_group(tiles[jt], here, jt), 0.0)
            total = piece if total is None else total + piece
        return total

    def repeated(rows, jt):
        return group_sum(jnp.where(group == jt, rows, 0.0))

    def before(rows):
        return jnp.where(group >= 1, pltpu.roll(rows, chans, 1), 0.0)

    def after(rows):
        return jnp.where(group < RUNS - 1, pltpu.roll(rows, 128 - chans, 1), 0.0)

    for copy in whole:
        copy.wait()
    for copy in keep:
        copy.start()
    for copy in small:
        copy.wait()
    pl.semaphore_wait(barrier, HALF)

    remote(filt.at[pl.ds(0, 3)], filt.at[pl.ds(3, 3)], 3, partner).start()

    def send_kv(slot, x, w, device):
        remote(proj_ref.at[pl.ds(1, 2), x, :, w], rx.at[my_slot, pl.ds(1, 2)], 0, device).start()

    def send_q_cot(slot, x, w, device):
        remote(proj_ref.at[0, x, :, w], rx.at[my_slot, 0], 1, device).start()
        remote(cot_ref.at[x, :, w], rx.at[my_slot, 3], 2, device).start()

    each_peer(send_kv)
    each_peer(send_q_cot)

    for i in range(3):
        rows = jnp.concatenate(
            [
                sw[i, :, pl.ds(pl.multiple_of(my_x * 128, 128), 128)],
                jnp.zeros((SUB - TAPS, 128), F32),
            ],
            axis=0,
        )
        rows = pltpu.roll(rows, lax.rem(128 - my_w * own, 128), 1)
        rows = jnp.where(lane < own, rows, 0.0) + pltpu.roll(
            jnp.where(jnp.logical_and(lane >= 64, lane < 64 + own), rows, 0.0), 64 + own, 1
        )
        rows = group_sum(rows)
        for j in range(TAPS):
            wt[TAPS * i + j] = jnp.broadcast_to(rows[j : j + 1, :], (SUB, 128))
    for copy in keep:
        copy.wait()
    arrived(filt.at[pl.ds(3, 3)], 3)
    par[...] = jnp.zeros_like(par)
    for k in range(2):
        mine, theirs = filt[k], filt[3 + k]
        first, second = jnp.where(is_a, mine, theirs), jnp.where(is_a, theirs, mine)
        for g in range(128 // chans):
            par[k, g * chans : g * chans + own, 0:MODES] = first
            par[k, g * chans + own : (g + 1) * chans, 0:MODES] = second
    mine, theirs = filt[2, 0:1, :], filt[5, 0:1, :]
    par[2, 0:1, 0:own] = jnp.where(is_a, mine, theirs)
    par[2, 1:2, 0:own] = jnp.where(is_a, theirs, mine)
    skip_row = group_sum(par[2, 0:1, :] + pltpu.roll(par[2, 1:2, :], own, 1))
    wt[9] = jnp.broadcast_to(skip_row, (SUB, 128))
    per = par[0].T[0:MODES, :] * (1.0 / length)
    residue = par[1].T[0:MODES, :]
    scale = jnp.sqrt(one_minus_exp(2.0 * per))
    coef_rows = residue * scale
    lam_rows = jnp.exp(-per)
    inv_lam = jnp.exp(per)
    par[3, 0:MODES, :] = per
    for m in range(MODES):
        lam[m] = jnp.broadcast_to(lam_rows[m : m + 1, :], (SUB, 128))
        coef[m] = jnp.broadcast_to(coef_rows[m : m + 1, :], (SUB, 128))

    def power(span):
        return jnp.exp(per * (-1.0 * span))

    sub_spans = [1, 2, 4]
    run_span, pair_span = power(run_len), power(2 * run_len)
    up_span = jnp.exp(per * (-1.0 * local_len) * group.astype(F32))
    down_span = jnp.exp(per * (-1.0 * local_len) * (WIDE - 1 - group).astype(F32))

    row = lax.broadcasted_iota(jnp.int32, (local_len, local_len), 0)
    column = lax.broadcasted_iota(jnp.int32, (local_len, local_len), 1)
    order = jnp.where(column == lax.rem(row, SUB) * steps + row // SUB, 1.0, 0.0).astype(BF16)

    def turn(arrays):
        def tile(jt):
            for a in arrays:
                block = rx[pl.ds(WIDE * jt, WIDE), a].reshape(128, local_len)
                rows = lax.dot_general(
                    order, block, (((1,), (1,)), ((), ())), preferred_element_type=F32
                ).reshape(steps, SUB, 128)
                xt[a, jt, RIM : RIM + steps] = rows
                if a < 3:
                    for i in range(RIM):
                        moved = pltpu.roll(rows[steps - RIM + i], 1, 0)
                        first = jnp.where(group == 0, 0.0, pltpu.roll(moved, chans, 1))
                        xt[a, jt, i] = jnp.where(sub_row == 0, first, moved)

        for jt in range(RUNS):
            tile(jt)

    def turn_back(rows):
        flat = rows.astype(BF16).reshape(local_len, 128)
        return (
            lax.dot_general(flat, order, (((0,), (0,)), ((), ())), preferred_element_type=F32)
            .astype(BF16)
            .reshape(WIDE, 2, own, local_len)
        )

    def path(a, jt, p):
        total = None
        for j in range(TAPS):
            term = wt[TAPS * a + j] * xt[a, jt, RIM + p - j]
            total = term if total is None else total + term
        return total

    def last_rows(a):
        return packed(
            [
                jnp.concatenate(
                    [xt[a, jt, steps + i, SUB - 1 : SUB, :] for i in range(RIM)], axis=0
                )
                for jt in range(RUNS)
            ],
            WIDE - 1,
        )

    def first_rows(a):
        return packed(
            [
                jnp.concatenate([xt[a, jt, RIM + i, 0:1, :] for i in range(RIM)], axis=0)
                for jt in range(RUNS)
            ],
            0,
        )

    def edge_path(a, first, last):
        w = [wt[TAPS * a + j][0:1, :] for j in range(TAPS)]
        return (
            w[0] * first[0:1] + w[1] * last[1:2] + w[2] * last[0:1],
            w[0] * first[1:2] + w[1] * first[0:1] + w[2] * last[1:2],
        )

    def mine_before(rows):
        return jnp.where(is_a, rows, before(rows))

    def theirs_before(rows):
        return jnp.where(is_a, before(rows), rows)

    def theirs_after(rows):
        return jnp.where(is_a, rows, after(rows))

    def fill_rim(a, rows):
        for jt in range(RUNS):
            rim = to_group(rows, jt, 0)
            for i in range(RIM):
                xt[a, jt, i] = jnp.where(
                    corner, jnp.broadcast_to(rim[i : i + 1, :], (SUB, 128)), xt[a, jt, i]
                )

    many = 8

    def block_ends(k, signal, reverse):
        def some(at, carry):
            jt = at // (MODES // many)
            first = lax.rem(at, MODES // many) * many
            lams = [lam[first + i] for i in range(many)]
            state = [None] * many
            for p in reversed(range(steps)) if reverse else range(steps):
                x = signal[jt, p]
                for i in range(many):
                    state[i] = x if state[i] is None else lams[i] * state[i] + x
            for i in range(many):
                pers = jnp.broadcast_to(par[3, pl.ds(first + i, 1), :], (SUB, 128))
                s = state[i]
                for d in sub_spans:
                    factor = jnp.exp(pers * (-1.0 * steps * d))
                    if reverse:
                        moved = jnp.where(sub_row < SUB - d, pltpu.roll(s, SUB - d, 0), 0.0)
                    else:
                        moved = jnp.where(sub_row >= d, pltpu.roll(s, d, 0), 0.0)
                    s = s + factor * moved
                if reverse:
                    ins[k, jt, first + i] = jnp.where(
                        sub_row < SUB - 1, pltpu.roll(s, SUB - 1, 0), 0.0
                    )
                    tots[k, jt, pl.ds(first + i, 1), :] = s[0:1, :]
                else:
                    ins[k, jt, first + i] = jnp.where(sub_row >= 1, pltpu.roll(s, 1, 0), 0.0)
                    tots[k, jt, pl.ds(first + i, 1), :] = s[SUB - 1 : SUB, :]
            return carry

        lax.fori_loop(0, RUNS * (MODES // many), some, 0)

    def run_ends(k, reverse):
        tiles = []
        for jt in range(RUNS):
            s = tots[k, jt]
            for d in (1, 2):
                if reverse:
                    moved = jnp.where(group < WIDE - d, pltpu.roll(s, 128 - chans * d, 1), 0.0)
                else:
                    moved = jnp.where(group >= d, pltpu.roll(s, chans * d, 1), 0.0)
                s = s + power(local_len * d) * moved
            tiles.append(s)
            tots[k, jt] = after(s) if reverse else before(s)
        return packed(tiles, 0 if reverse else WIDE - 1)

    arrived(rx.at[pl.ds(0, HALF - 1), pl.ds(1, 2)], 0)
    turn((1, 2))

    def gate_kv(jt, carry):
        for p in range(steps):
            key, value = path(1, jt, p), path(2, jt, p)
            u = rounded(key * value)
            ks[jt, p] = key
            vs[jt, p] = value
            us[jt, p] = jnp.where(corner, 0.0, u) if p < 2 else u
        return carry

    lax.fori_loop(0, RUNS, gate_kv, 0)
    block_ends(0, us, False)
    my_f = run_ends(0, False)
    k_last, v_last = last_rows(1), last_rows(2)
    k_first, v_first = first_rows(1), first_rows(2)
    edge[0, 0:MODES, :] = my_f
    edge[0, MODES : MODES + 8, :] = jnp.concatenate([k_last, v_last, k_first, v_first], axis=0)
    remote(edge.at[0], edge_in.at[0], 4, partner).start()

    arrived(rx.at[pl.ds(0, HALF - 1), 0], 1)
    arrived(rx.at[pl.ds(0, HALF - 1), 3], 2)
    turn((0, 3))

    def gate_q(jt, carry):
        for p in range(steps):
            query = path(0, jt, p)
            g = rounded(xt[3, jt, RIM + p] * query)
            qs[jt, p] = query
            gs[jt, p] = jnp.where(corner, 0.0, g) if p < 2 else g
        return carry

    q_last, q_first, c_first = last_rows(0), first_rows(0), first_rows(3)
    edge[1, MODES : MODES + 8, :] = jnp.concatenate(
        [q_last, q_first, c_first, jnp.zeros((2, 128), F32)], axis=0
    )
    remote(
        edge.at[1, pl.ds(MODES, 8)], edge_in.at[1, pl.ds(MODES, 8)], 10, partner
    ).start()
    lax.fori_loop(0, RUNS, gate_q, 0)
    block_ends(1, gs, True)
    my_b = run_ends(1, True)
    edge[1, 0:MODES, :] = my_b
    remote(edge.at[1, pl.ds(0, MODES)], edge_in.at[1, pl.ds(0, MODES)], 5, partner).start()

    arrived(edge_in.at[0], 4)
    their_f = edge_in[0, 0:MODES, :]
    rows = edge_in[0, MODES : MODES + 8, :]
    tk_last, tv_last, tk_first, tv_first = rows[0:2], rows[2:4], rows[4:6], rows[6:8]
    fill_rim(1, theirs_before(tk_last))
    fill_rim(2, theirs_before(tv_last))

    def regate_kv(jt, carry):
        for p in range(2):
            key, value = path(1, jt, p), path(2, jt, p)
            ks[jt, p] = key
            vs[jt, p] = value
            us[jt, p] = rounded(key * value)
        return carry

    for jt in range(RUNS):
        regate_kv(jt, 0)
    my_k = edge_path(1, k_first, theirs_before(tk_last))
    my_v = edge_path(2, v_first, theirs_before(tv_last))
    their_k = edge_path(1, tk_first, mine_before(k_last))
    their_v = edge_path(2, tv_first, mine_before(v_last))
    my_u = [rounded(k * v) for k, v in zip(my_k, my_v)]
    their_u = [rounded(k * v) for k, v in zip(their_k, their_v)]
    late = (power(run_len - 1), power(run_len - 2))
    my_f = my_f + late[0] * my_u[0] + late[1] * my_u[1]
    their_f = their_f + late[0] * their_u[0] + late[1] * their_u[1]
    a_f, b_f = jnp.where(is_a, my_f, their_f), jnp.where(is_a, their_f, my_f)
    scan = run_span * a_f + b_f
    scan = scan + pair_span * before(scan)
    scan = scan + power(4 * run_len) * jnp.where(group >= 2, pltpu.roll(scan, 2 * chans, 1), 0.0)
    into_a = before(scan)
    carry_f = jnp.where(is_a, into_a, run_span * into_a + a_f)
    next_f = run_span * carry_f + my_f
    whole_f = carry_f + inv_lam * (my_u[0] + inv_lam * my_u[1])
    for jt in range(RUNS):
        tots[0, jt] = tots[0, jt] + up_span * repeated(whole_f, jt)
        ends[jt] = repeated(carry_f, jt)

    def in_state(k, jt, m):
        pers = jnp.broadcast_to(par[3, pl.ds(m, 1), :], (SUB, 128))
        into = jnp.broadcast_to(tots[k, jt, pl.ds(m, 1), :], (SUB, 128))
        away = (sub_row if k == 0 else SUB - 1 - sub_row).astype(F32)
        state = ins[k, jt, m] + jnp.exp(pers * (-1.0 * steps) * away) * into
        if k == 0:
            exact = jnp.broadcast_to(ends[jt, pl.ds(m, 1), :], (SUB, 128))
            state = jnp.where(corner, exact, state)
        return state

    def summed(parts):
        while len(parts) > 1:
            parts = [parts[i] + parts[i + 1] for i in range(0, len(parts), 2)]
        return parts[0]

    def conv_tile(jt, carry):
        def some(at, totals):
            totals = list(totals)
            first = at * many
            lams = [lam[first + i] for i in range(many)]
            coefs = [coef[first + i] for i in range(many)]
            state = [in_state(0, jt, first + i) for i in range(many)]
            for p in range(steps):
                u = us[jt, p]
                for i in range(many):
                    state[i] = lams[i] * state[i] + u
                    kept[jt, first + i, p] = state[i]
                totals[p] = totals[p] + summed([coefs[i] * state[i] for i in range(many)])
            return tuple(totals)

        start = tuple(wt[9] * us[jt, p] for p in range(steps))
        totals = lax.fori_loop(0, MODES // many, some, start)
        for p in range(steps):
            cv[jt, p] = rounded(totals[p])
        return carry

    lax.fori_loop(0, RUNS, conv_tile, 0)

    arrived(edge_in.at[1, pl.ds(MODES, 8)], 10)
    rows = edge_in[1, MODES : MODES + 8, :]
    tq_last, tq_first, tc_first = rows[0:2], rows[2:4], rows[4:6]
    fill_rim(0, theirs_before(tq_last))

    def regate_q(jt, carry):
        for p in range(2):
            query = path(0, jt, p)
            qs[jt, p] = query
            gs[jt, p] = rounded(xt[3, jt, RIM + p] * query)
        for p in range(steps):
            gf[0, jt, p] = xt[3, jt, RIM + p] * cv[jt, p]
        return carry

    for jt in range(RUNS):
        regate_q(jt, 0)
    next_u = [theirs_after(u) for u in their_u]
    next_c = theirs_after(tc_first)
    state0 = lam_rows * next_f + next_u[0]
    state1 = lam_rows * state0 + next_u[1]
    beyond = [[], [], []]
    for i, state in enumerate((state0, state1)):
        conv = rounded(
            jnp.sum(coef_rows * state, axis=0, keepdims=True) + skip_row * next_u[i]
        )
        beyond[0].append(next_c[i : i + 1] * conv)

    def gf_rim(a):
        for jt in range(RUNS):
            for i in range(RIM):
                rim = jnp.broadcast_to(to_group(beyond[a][i], jt, WIDE - 1), (SUB, 128))
                moved = pltpu.roll(gf[a, jt, i], SUB - 1, 0)
                last = jnp.where(group == WIDE - 1, rim, pltpu.roll(moved, 128 - chans, 1))
                gf[a, jt, steps + i] = jnp.where(sub_row == SUB - 1, last, moved)

    def grad_path(a, jt):
        w = [wt[TAPS * a + j] for j in range(TAPS)]
        rows = []
        for p in range(steps):
            total = w[0] * gf[a, jt, p]
            for j in range(1, TAPS):
                total = total + w[j] * gf[a, jt, p + j]
            rows.append(total)
        so[pl.ds(WIDE * jt, WIDE), 1 + a] = turn_back(jnp.stack(rows))

    def send_tile(jt, arrays, k):
        for w in range(WIDE):
            slot = WIDE * jt + w

            @pl.when(slot != my_slot)
            def _():
                remote(
                    so.at[slot, arrays],
                    land.at[my_slot, arrays],
                    k,
                    (2 * jt + side) * WIDE + w,
                ).start()

    gf_rim(0)

    def first_results(t, carry):
        jt = lax.rem(my_x + 1 + t, RUNS)
        so[pl.ds(WIDE * jt, WIDE), 0] = turn_back(
            jnp.stack([qs[jt, p] * cv[jt, p] for p in range(steps)])
        )
        grad_path(0, jt)
        send_tile(jt, pl.ds(0, 2), 7)
        return carry

    for t in range(RUNS):
        first_results(t, 0)

    my_q = edge_path(0, q_first, theirs_before(tq_last))
    their_q = edge_path(0, tq_first, mine_before(q_last))
    my_g = [rounded(my_q[i] * c_first[i : i + 1]) for i in range(2)]
    their_g = [rounded(their_q[i] * tc_first[i : i + 1]) for i in range(2)]
    arrived(edge_in.at[1, pl.ds(0, MODES)], 5)
    their_b = edge_in[1, 0:MODES, :]
    my_b = my_b + my_g[0] + lam_rows * my_g[1]
    their_b = their_b + their_g[0] + lam_rows * their_g[1]
    a_b, b_b = jnp.where(is_a, my_b, their_b), jnp.where(is_a, their_b, my_b)
    scan = a_b + run_span * b_b
    scan = scan + pair_span * after(scan)
    scan = scan + power(4 * run_len) * jnp.where(
        group < RUNS - 2, pltpu.roll(scan, 128 - 2 * chans, 1), 0.0
    )
    into_b = after(scan)
    carry_b = jnp.where(is_a, run_span * into_b + b_b, into_b)
    for jt in range(RUNS):
        tots[1, jt] = tots[1, jt] + down_span * repeated(carry_b, jt)

    next_g = [theirs_after(g) for g in their_g]
    for i, back in enumerate((carry_b, inv_lam * (carry_b - next_g[0]))):
        back = rounded(jnp.sum(coef_rows * back, axis=0, keepdims=True) + skip_row * next_g[i])
        beyond[1].append(back * theirs_after(their_v[i]))
        beyond[2].append(back * theirs_after(their_k[i]))

    def back_tile(jt, carry):
        def some(at, totals):
            totals = list(totals)
            first = at * many
            lams = [lam[first + i] for i in range(many)]
            coefs = [coef[first + i] for i in range(many)]
            state = [in_state(1, jt, first + i) for i in range(many)]
            for i in range(many):
                ins[1, jt, first + i] = state[i]
            for p in reversed(range(steps)):
                g = gs[jt, p]
                for i in range(many):
                    state[i] = lams[i] * state[i] + g
                totals[p] = totals[p] + summed([coefs[i] * state[i] for i in range(many)])
            return tuple(totals)

        carry = list(carry)
        start = tuple(wt[9] * gs[jt, p] for p in range(steps))
        totals = lax.fori_loop(0, MODES // many, some, start)
        for p in range(steps):
            back = rounded(totals[p])
            grads = (gf[0, jt, p], back * vs[jt, p], back * ks[jt, p])
            gf[1, jt, p] = grads[1]
            gf[2, jt, p] = grads[2]
            for a in range(3):
                for j in range(TAPS):
                    carry[TAPS * a + j] += grads[a] * xt[a, jt, RIM + p - j]
            carry[9] += us[jt, p] * gs[jt, p]
        return tuple(carry)

    found = lax.fori_loop(
        0, RUNS, back_tile, tuple(jnp.zeros((SUB, 128), F32) for _ in range(10))
    )

    taps = [group_sum(jnp.sum(part, axis=0, keepdims=True)) * (1.0 / root) for part in found]
    sides = []
    for r in range(3):
        side_row = jnp.zeros((1, 128), F32)
        for g in range(4):
            if 4 * r + g < 3 * TAPS:
                side_row = jnp.where(group == g, taps[4 * r + g], side_row)
        sides.append(side_row)
    shorts[...] = jnp.concatenate(sides + [jnp.zeros((1, 128), F32)], axis=0)

    def send_short(t, carry):
        remote(shorts, all_short.at[me], 9, lax.rem(me + t, n)).start()
        return carry

    gf_rim(1)
    gf_rim(2)

    def last_results(t, carry):
        @pl.when(t < 2)
        def _():
            lax.fori_loop(jnp.maximum(16 * t, 1), 16 * t + 16, send_short, 0)

        jt = lax.rem(my_x + 1 + t, RUNS)
        grad_path(1, jt)
        grad_path(2, jt)
        send_tile(jt, pl.ds(2, 2), 8)
        return carry

    lax.fori_loop(0, RUNS, last_results, 0)
    keep_out = [pltpu.make_async_copy(so.at[my_slot], land.at[my_slot], local_sem.at[0])]
    keep_out[0].start()

    pacc[...] = jnp.zeros_like(pacc)
    racc[...] = jnp.zeros_like(racc)
    few = 4

    def mode_sums(at, carry):
        jt = at // (MODES // few)
        first = lax.rem(at, MODES // few) * few
        lams = [lam[first + i] for i in range(few)]
        state = [ins[1, jt, first + i] for i in range(few)]
        plain = [None] * few
        ramped = [None] * few
        for p in reversed(range(steps)):
            g = gs[jt, p]
            for i in range(few):
                fwd = kept[jt, first + i, p]
                flat = g * fwd
                ramp = state[i] * fwd
                plain[i] = flat if plain[i] is None else plain[i] + flat
                ramped[i] = ramp if ramped[i] is None else ramped[i] + ramp
                state[i] = lams[i] * state[i] + g
        for i in range(few):
            pacc[first + i] += plain[i]
            racc[first + i] += ramped[i]
        return carry

    lax.fori_loop(0, RUNS * (MODES // few), mode_sums, 0)
    my_plain = group_sum(
        jnp.concatenate([jnp.sum(pacc[m], axis=0, keepdims=True) for m in range(MODES)], axis=0)
    )
    my_ramped = group_sum(
        jnp.concatenate([jnp.sum(racc[m], axis=0, keepdims=True) for m in range(MODES)], axis=0)
    )
    sums[0:MODES, :] = my_plain
    sums[MODES : 2 * MODES, :] = my_ramped
    sums[2 * MODES : 2 * MODES + 8, :] = jnp.broadcast_to(taps[9], (SUB, 128))
    remote(sums, sums_in, 6, partner).start()

    arrived(sums_in, 6)
    plain = my_plain + sums_in[0:MODES, :]
    ramped = lam_rows * (my_ramped + sums_in[MODES : 2 * MODES, :])
    skips = taps[9] + sums_in[2 * MODES : 2 * MODES + 1, :]
    gskip[...] = jnp.where(is_a, skips[:, 0:own], skips[:, own : 2 * own])
    grad_res = scale * plain / root
    grad_dec = residue * (jnp.exp(-2.0 * per) / scale * plain - scale * ramped) / (length * root)
    par[0, 0:MODES, :] = grad_res
    par[1, 0:MODES, :] = grad_dec
    for k in range(2):
        turned = par[k].T
        gres[k] = jnp.where(is_a, turned[0:own, 0:MODES], turned[own : 2 * own, 0:MODES])
    for at, (src, dst) in enumerate(
        (
            (shorts, all_short.at[me]),
            (gres.at[0], gres_hbm),
            (gres.at[1], gdec_hbm),
            (gskip, gskip_hbm),
        )
    ):
        keep_out.append(pltpu.make_async_copy(src, dst, local_sem.at[1 + at]))
        keep_out[-1].start()

    arrived(all_short.at[pl.ds(0, n - 1)], 9)
    for copy in keep_out:
        copy.wait()
    most = pl.ds(0, HALF - 1)
    arrived(so.at[most, pl.ds(0, 2)], 7)
    arrived(so.at[most, pl.ds(2, 2)], 8)
    left(rx.at[most, pl.ds(1, 2)], 0)
    left(rx.at[most, 0], 1)
    left(rx.at[most, 3], 2)
    left(filt.at[pl.ds(0, 3)], 3)
    left(edge.at[0], 4)
    left(edge.at[1, pl.ds(0, MODES)], 5)
    left(edge.at[1, pl.ds(MODES, 8)], 10)
    left(sums, 6)
    left(so.at[most, pl.ds(0, 2)], 7)
    left(so.at[most, pl.ds(2, 2)], 8)
    left(all_short.at[pl.ds(0, n - 1)], 9)


def write_out(land, parts, res, dec, skip, out, gproj, gshort, gres, gdec, gskip):
    own = land.shape[3]
    place = lax.broadcasted_iota(jnp.int32, (1, 128), 1) // own
    for x in range(RUNS):
        for half in range(2):
            for w in range(WIDE):
                out[x, half, w] = land[WIDE * x + w, 0, half]
                for a in range(3):
                    gproj[a, x, half, w] = land[WIDE * x + w, 1 + a, half]
        rows = [jnp.zeros((4, 128), F32) for _ in range(4)]
        for w in range(WIDE):
            at = 2 * WIDE * x + w
            both = parts[at] + parts[at + WIDE]
            for g in range(4):
                low = (own * w - 2 * own * g) % 128
                high = (64 + own * w - own - 2 * own * g) % 128
                low = pltpu.roll(both, low, 1) if low else both
                high = pltpu.roll(both, high, 1) if high else both
                rows[g] = jnp.where(place == w, low, jnp.where(place == w + WIDE, high, rows[g]))
        for k in range(3 * TAPS):
            gshort[k // TAPS, k % TAPS : k % TAPS + 1, 128 * x : 128 * (x + 1)] = rows[k % 4][
                k // 4 : k // 4 + 1, :
            ]
    gres[...] = res[...]
    gdec[...] = dec[...]
    gskip[...] = skip[...]


def per_device(projected, short_weight, residues, decay_rates, skip_weight, cotangent):
    n = lax.axis_size("context")
    channels, local_len = cotangent.shape
    own = channels // n
    steps = local_len // SUB
    vmem = pl.BlockSpec(memory_space=pltpu.VMEM)
    hbm = pl.BlockSpec(memory_space=pltpu.HBM)
    stepped = pltpu.VMEM((RUNS, steps, SUB, 128), F32)
    blocks = (RUNS, 2, WIDE, own, local_len)
    small = (
        jax.ShapeDtypeStruct((own, MODES), F32),
        jax.ShapeDtypeStruct((own, MODES), F32),
        jax.ShapeDtypeStruct((1, own), F32),
    )
    results = pl.pallas_call(
        functools.partial(kernel, n, local_len, own),
        out_shape=(
            jax.ShapeDtypeStruct((HALF, 4, 2, own, local_len), BF16),
            jax.ShapeDtypeStruct((n, 4, 128), F32),
        )
        + small,
        in_specs=[hbm] * 6,
        out_specs=(hbm,) * 5,
        scratch_shapes=[
            pltpu.VMEM((3,) + blocks, BF16),
            pltpu.VMEM(blocks, BF16),
            pltpu.VMEM((HALF, 4, 2, own, local_len), BF16),
            pltpu.VMEM((HALF, 4, 2, own, local_len), BF16),
            pltpu.VMEM((4, RUNS, RIM + steps, SUB, 128), F32),
            stepped,
            stepped,
            stepped,
            stepped,
            stepped,
            stepped,
            pltpu.VMEM((3, RUNS, steps + RIM, SUB, 128), F32),
            pltpu.VMEM((RUNS, MODES, steps, SUB, 128), F32),
            pltpu.VMEM((3, TAPS, channels), F32),
            pltpu.VMEM((6, own, MODES), F32),
            pltpu.VMEM((4, 128, 128), F32),
            pltpu.VMEM((10, SUB, 128), F32),
            pltpu.VMEM((MODES, SUB, 128), F32),
            pltpu.VMEM((MODES, SUB, 128), F32),
            pltpu.VMEM((2, RUNS, MODES, 128), F32),
            pltpu.VMEM((2, RUNS, MODES, SUB, 128), F32),
            pltpu.VMEM((RUNS, MODES, 128), F32),
            pltpu.VMEM((2, MODES + 8, 128), F32),
            pltpu.VMEM((2, MODES + 8, 128), F32),
            pltpu.VMEM((8 + 2 * MODES, 128), F32),
            pltpu.VMEM((8 + 2 * MODES, 128), F32),
            pltpu.VMEM((4, 128), F32),
            pltpu.VMEM((2, own, MODES), F32),
            pltpu.VMEM((1, own), F32),
            pltpu.VMEM((MODES, SUB, 128), F32),
            pltpu.VMEM((MODES, SUB, 128), F32),
            pltpu.SemaphoreType.DMA((11,)),
            pltpu.SemaphoreType.DMA((11,)),
            pltpu.SemaphoreType.DMA((8,)),
        ],
        compiler_params=pltpu.CompilerParams(
            collective_id=0, has_side_effects=True, vmem_limit_bytes=56 * 1024 * 1024
        ),
    )(
        projected.reshape((3,) + blocks),
        cotangent.reshape(blocks),
        short_weight.transpose(0, 2, 1),
        decay_rates,
        residues,
        skip_weight.reshape(1, -1),
    )
    output, grad_projected, grad_short, grad_res, grad_dec, grad_skip = pl.pallas_call(
        write_out,
        out_shape=(
            jax.ShapeDtypeStruct(blocks, BF16),
            jax.ShapeDtypeStruct((3,) + blocks, BF16),
            jax.ShapeDtypeStruct((3, TAPS, channels), F32),
        )
        + small,
        in_specs=[vmem] * 5,
        out_specs=(vmem,) * 6,
    )(*results)
    return (
        output.reshape(channels, local_len),
        grad_projected.reshape(3, channels, local_len),
        grad_short.transpose(0, 2, 1),
        grad_res,
        grad_dec,
        grad_skip.reshape(-1),
    )


def solution(mesh):
    return jax.shard_map(
        per_device,
        mesh=mesh,
        in_specs=(
            P(None, "tensor", "context"),
            P(None, "tensor", None),
            P(("tensor", "context"), None),
            P(("tensor", "context"), None),
            P(("tensor", "context")),
            P("tensor", "context"),
        ),
        out_specs=(
            P("tensor", "context"),
            P(None, "tensor", "context"),
            P(None, "tensor", None),
            P(("tensor", "context"), None),
            P(("tensor", "context"), None),
            P(("tensor", "context")),
        ),
        check_vma=False,
    )
```
